512 devices in a mesh: space: 32 (over z, x), brow: 8 (over y), bcol: 2 (over core).
Axes of the slice: x: 4, y: 8, z: 8, core: 2. Of those that a mesh axis runs over, the one named last changes fastest.
Arguments:
- orbitals: float32 [589824, 256], P(('space', 'brow'), 'bcol'), may hold values from -0.0078125 to 0.0078125
- applied: float32 [589824, 256], P(('space', 'brow'), 'bcol'), may hold values from -0.0078125 to 0.0078125
- cotangent: float32 [589824, 256], P(('space', 'brow'), 'bcol'), may hold values from -6 to 6
- rotation: float32 [256, 256], P('brow', 'bcol'), may hold values from -0.5 to 1.5, as said below
- levels: float32 [256], replicated, may hold values from -3 to 9.8, as said below
Outputs:
- orbital_grad: float32 [589824, 256], P(('space', 'brow'), 'bcol')
The draws below stay inside these ranges and needn't reach their ends.
Inputs may be any that keep to these rules, and one draw needn't show every extreme that they name: rotation has a unit diagonal plus independent entries of deviation 0.4 / sqrt(256). levels rise with the index, neighbours at least 0.025 apart.
All inputs are finite; a program needn't handle non-finite values.
Results may differ from the reference program's by a relative error of at most 0.0003.
Values sent between devices are 32-bit elements; how exact they have to be, the bound alone decides.
No kernel may reach another device: no remote copies, remote signals or barrier semaphores. Data moves between devices by JAX's collectives and lax.ppermute only.
A program may use at most 64 MiB of HBM per device.

```python
import jax
import jax.numpy as jnp
from jax import lax

BANDS = 256
CELLS = 589824


def draw_rotation(key, part):
    key = jax.random.fold_in(key, 11)
    noise = jnp.clip(jax.random.normal(key, (BANDS, BANDS), jnp.float32), -3.0, 3.0)
    rows = jnp.arange(BANDS)[:, None]
    cols = jnp.arange(BANDS)[None, :]
    unit = jnp.where(rows == cols, 1.0, 0.0).astype(jnp.float32)
    return unit + noise * (0.4 / jnp.sqrt(jnp.float32(BANDS)))


def draw_levels(key, part):
    key = jax.random.fold_in(key, 23)
    jitter = jax.random.uniform(key, (BANDS,), jnp.float32)
    steps = jnp.arange(BANDS).astype(jnp.float32)
    return 0.05 * steps + 0.025 * jitter - 3.0


def steps_of(stream_key, dims, split, low, top_value):
    def one(axis_at, blocks):
        draws = jax.random.uniform(jax.random.fold_in(jax.random.fold_in(stream_key, 6), axis_at), (blocks,), jnp.float32, low / len(split), top_value / len(split))
        return jnp.repeat(jnp.exp(draws), dims[axis_at] // blocks).reshape((-1,) + (1,) * (len(dims) - axis_at - 1))

    gain = one(*split[0])
    for cut in split[1:]:
        gain = gain * one(*cut)
    return gain


def scatter_about(stream_key, shape, width, limit, shards=(), kind=jnp.bfloat16):
    loudness = steps_of(stream_key, shape, shards, -0.22, 0.18) if shards else 1.0
    array = jax.random.normal(stream_key, shape, jnp.float32) * width * loudness
    return jnp.minimum(jnp.maximum(array, -limit), limit).astype(kind)


def setup_inputs(seed: int = 0) -> dict:
    arg_keys = jax.random.split(jax.random.key(seed), 6)
    return {
        "orbitals": scatter_about(arg_keys[0], (CELLS, BANDS), CELLS ** -0.5, 0.0078125, ((0, 256), (1, 2)), jnp.float32),
        "applied": scatter_about(arg_keys[1], (CELLS, BANDS), CELLS ** -0.5, 0.0078125, ((0, 256), (1, 2)), jnp.float32),
        "cotangent": scatter_about(arg_keys[2], (CELLS, BANDS), 1.0, 6.0, ((0, 256), (1, 2)), jnp.float32),
        "rotation": draw_rotation(jax.random.fold_in(arg_keys[5], 71), 0),
        "levels": draw_levels(jax.random.fold_in(arg_keys[5], 71), 0),
    }


def matmul(left, right):
    return jnp.dot(left, right, preferred_element_type=jnp.float32, precision=lax.Precision.HIGHEST)


def subspace(rotation, levels, grad_rot):
    gram_rot = matmul(rotation.T, grad_rot)
    level_gaps = levels[None, :] - levels[:, None]
    diag_mask = jnp.eye(levels.shape[0], dtype=bool)
    inverse = jnp.where(diag_mask, jnp.float32(0.0), 1.0 / jnp.where(diag_mask, jnp.float32(1.0), level_gaps))
    mixing = inverse * gram_rot
    sym_ham = mixing + mixing.T
    sym_ovl = mixing * levels[None, :] + levels[:, None] * mixing.T + jnp.diag(jnp.diag(gram_rot))
    ham_coef = matmul(matmul(rotation, sym_ham), rotation.T)
    ovl_coef = -matmul(matmul(rotation, sym_ovl), rotation.T)
    return ham_coef, ovl_coef


def reference(orbitals, applied, cotangent, rotation, levels):
    grad_rot = matmul(orbitals.T, cotangent)
    ham_coef, ovl_coef = subspace(rotation, levels, grad_rot)
    return matmul(orbitals, ovl_coef) + matmul(applied, ham_coef) + matmul(cotangent, rotation.T)
```

```python
import functools

import jax
import jax.numpy as jnp
from jax import lax
from jax.experimental import pallas as pl
from jax.experimental.pallas import tpu as pltpu
from jax.sharding import PartitionSpec as P

F32 = jnp.float32
BF16 = jnp.bfloat16
VMEM = pl.BlockSpec(memory_space=pltpu.VMEM)
ANY = pl.BlockSpec(memory_space=pl.ANY)
CHUNK = 576


def halves(x):
    high = x.astype(BF16)
    return high, (x - high.astype(F32)).astype(BF16)


def dot(left, right, dims, precision=None):
    return lax.dot_general(
        left, right, (dims, ((), ())), preferred_element_type=F32, precision=precision
    )


def exact(left, right, dims=((1,), (0,))):
    return dot(left, right, dims, lax.Precision.HIGHEST)


def gram_kernel(bcol_ref, own_hbm, oth_hbm, cot_hbm, out_ref, own, oth, cot, sems):
    cells, width = own.shape
    steps = cells // CHUNK
    copies = []
    for step in range(steps):
        rows = pl.ds(step * CHUNK, CHUNK)
        group = [
            pltpu.make_async_copy(src.at[rows], dst.at[rows], sems.at[step, at])
            for at, (src, dst) in enumerate(((own_hbm, own), (oth_hbm, oth), (cot_hbm, cot)))
        ]
        for copy in group:
            copy.start()
        copies.append(group)
    total = None
    for step in range(steps):
        rows = pl.ds(step * CHUNK, CHUNK)
        for copy in copies[step]:
            copy.wait()
        cot_high, cot_low = halves(cot[rows, :])
        own_high, own_low = halves(own[rows, :])
        oth_high, oth_low = halves(oth[rows, :])
        high = jnp.concatenate([own_high, oth_high], axis=1)
        low = jnp.concatenate([own_low, oth_low], axis=1)
        cells_first = ((0,), (0,))
        part = (
            dot(cot_high, high, cells_first)
            + dot(cot_low, high, cells_first)
            + dot(cot_high, low, cells_first)
        )
        total = part if total is None else total + part
    mine = bcol_ref[0]
    out_ref[pl.ds(pl.multiple_of(mine * width, width), width), :] = total[:, :width]
    out_ref[pl.ds(pl.multiple_of((1 - mine) * width, width), width), :] = total[:, width:]


def spread_kernel(parts_ref, panel_ref, out_ref):
    tile = jnp.sum(parts_ref[...], axis=0)
    both = jnp.concatenate([tile, panel_ref[...]], axis=0)
    out_ref[...] = jnp.broadcast_to(both[None], out_ref.shape)


def gather_kernel(parts_ref, out_ref):
    tiles = jnp.sum(parts_ref[:, :, :8, :], axis=0)
    both = tiles.reshape(16, tiles.shape[-1])
    out_ref[...] = jnp.broadcast_to(both[None], out_ref.shape)


def tail_kernel(
    bcol_ref,
    sums_ref,
    panels_ref,
    row_ref,
    col_ref,
    orb_own,
    orb_oth,
    app_own,
    app_oth,
    cot_own,
    cot_oth,
    out_hbm,
    held,
    result,
    weights,
    rotation_ref,
    in_sems,
    out_sems,
):
    sources = (orb_own, orb_oth, app_own, app_oth, cot_own, cot_oth)
    cells, width = result.shape
    steps = cells // CHUNK
    copies = []
    for step in range(steps):
        rows = pl.ds(step * CHUNK, CHUNK)
        group = [
            pltpu.make_async_copy(src.at[rows], held.at[at, rows], in_sems.at[step, at])
            for at, src in enumerate(sources)
        ]
        for copy in group:
            copy.start()
        copies.append(group)

    mine = bcol_ref[0]
    bands = 2 * width
    tiles = width // 8
    grad_t = jnp.concatenate(
        [
            jnp.concatenate(
                [
                    sums_ref[b * tiles : (b + 1) * tiles, c * 8 : (c + 1) * 8, :].reshape(width, width)
                    for b in range(2)
                ],
                axis=1,
            )
            for c in range(2)
        ],
        axis=0,
    )
    rotation = jnp.concatenate(
        [panels_ref[:, c, 8:, :].reshape(bands, width) for c in range(2)], axis=1
    )
    rotation_ref[...] = rotation
    gram_t = exact(grad_t, rotation)
    levels_row = row_ref[...]
    levels_col = col_ref[...]
    at_row = lax.broadcasted_iota(jnp.int32, (bands, bands), 0)
    at_col = lax.broadcasted_iota(jnp.int32, (bands, bands), 1)
    diagonal = at_row == at_col
    gaps = jnp.where(diagonal, 1.0, levels_col - levels_row)
    mixing_t = jnp.where(diagonal, 0.0, (1.0 / gaps) * gram_t)
    sym_ham = mixing_t + mixing_t.T
    scaled = levels_col * mixing_t
    sym_ovl = scaled + scaled.T + jnp.where(diagonal, gram_t, 0.0)
    rot_rows = rotation_ref[pl.ds(pl.multiple_of(mine * width, width), width), :]
    right = exact(jnp.concatenate([sym_ovl, sym_ham], axis=0), rot_rows, ((1,), (1,)))
    coefs = exact(rotation, jnp.concatenate([-right[:bands], right[bands:]], axis=1))
    rot_t = rot_rows.T
    for at, block in enumerate((coefs[:, :width], coefs[:, width:], rot_t)):
        high, low = halves(block)
        both = jnp.concatenate([high, low], axis=1)
        weights[at] = both

    first = pl.ds(pl.multiple_of(mine * width, width), width)
    second = pl.ds(pl.multiple_of((1 - mine) * width, width), width)
    weight = jnp.concatenate(
        [weights[at, rows, :] for at in range(3) for rows in (first, second)], axis=0
    )
    outs = []
    for step in range(steps):
        rows = pl.ds(step * CHUNK, CHUNK)
        for copy in copies[step]:
            copy.wait()
        left = jnp.concatenate([held[at, rows, :] for at in range(6)], axis=1)
        high, low = halves(left)
        inner = ((1,), (0,))
        wide = dot(high, weight, inner)
        result[rows, :] = wide[:, :width] + wide[:, width:] + dot(low, weight[:, :width], inner)
        copy = pltpu.make_async_copy(result.at[rows], out_hbm.at[rows], out_sems.at[step])
        copy.start()
        outs.append(copy)
    for copy in outs:
        copy.wait()


def body(orbitals, applied, cotangent, panel, levels):
    cells, width = orbitals.shape
    bands = 2 * width
    steps = cells // CHUNK
    swap = [(0, 1), (1, 0)]
    orb_oth = lax.ppermute(orbitals, "bcol", swap)
    app_oth = lax.ppermute(applied, "bcol", swap)
    cot_oth = lax.ppermute(cotangent, "bcol", swap)
    mine = lax.axis_index("bcol").reshape(1)
    smem = pl.BlockSpec(memory_space=pltpu.SMEM)
    space = lax.axis_size("space")
    brow = lax.axis_size("brow")
    tile = bands // space

    partial = pl.pallas_call(
        gram_kernel,
        out_shape=jax.ShapeDtypeStruct((bands, width), F32),
        in_specs=[smem, ANY, ANY, ANY],
        out_specs=VMEM,
        scratch_shapes=[pltpu.VMEM((cells, width), F32)] * 3 + [pltpu.SemaphoreType.DMA((steps, 3))],
        compiler_params=pltpu.CompilerParams(vmem_limit_bytes=24 * 2**20),
        name="gram",
    )(mine, orbitals, orb_oth, cotangent)

    parts = lax.all_to_all(partial.reshape(space, tile, width), "space", 0, 0, tiled=True)
    rows = tile + panel.shape[0]
    spread = pl.pallas_call(
        spread_kernel,
        out_shape=jax.ShapeDtypeStruct((2 * brow, rows, width), F32),
        in_specs=[VMEM, VMEM],
        out_specs=VMEM,
        name="spread",
    )(parts, panel)
    panels = lax.all_to_all(spread, ("brow", "bcol"), 0, 0, tiled=True)
    panels = panels.reshape(brow, 2, rows, width)
    gather = pl.pallas_call(
        gather_kernel,
        out_shape=jax.ShapeDtypeStruct((space, 2 * tile, width), F32),
        in_specs=[VMEM],
        out_specs=VMEM,
        name="gather",
    )(panels)
    sums = lax.all_to_all(gather, "space", 0, 0, tiled=True)

    return pl.pallas_call(
        tail_kernel,
        out_shape=jax.ShapeDtypeStruct((cells, width), F32),
        in_specs=[smem] + [VMEM] * 4 + [ANY] * 6,
        out_specs=ANY,
        scratch_shapes=[
            pltpu.VMEM((6, cells, width), F32),
            pltpu.VMEM((cells, width), F32),
            pltpu.VMEM((3, bands, bands), BF16),
            pltpu.VMEM((bands, bands), F32),
            pltpu.SemaphoreType.DMA((steps, 6)),
            pltpu.SemaphoreType.DMA((steps,)),
        ],
        compiler_params=pltpu.CompilerParams(vmem_limit_bytes=40 * 2**20),
        name="tail",
    )(
        mine,
        sums,
        panels,
        levels.reshape(1, bands),
        levels.reshape(bands, 1),
        orbitals,
        orb_oth,
        applied,
        app_oth,
        cotangent,
        cot_oth,
    )


def solution(mesh):
    return jax.shard_map(
        body,
        mesh=mesh,
        in_specs=(
            P(("space", "brow"), "bcol"),
            P(("space", "brow"), "bcol"),
            P(("space", "brow"), "bcol"),
            P("brow", "bcol"),
            P(),
        ),
        out_specs=P(("space", "brow"), "bcol"),
        check_vma=False,
    )
```

```python
import jax
import jax.numpy as jnp
from jax import lax
from jax.experimental import pallas as pl
from jax.experimental.pallas import tpu as pltpu
from jax.sharding import PartitionSpec as P

F32 = jnp.float32
BF16 = jnp.bfloat16
VMEM = pl.BlockSpec(memory_space=pltpu.VMEM)
SMEM = pl.BlockSpec(memory_space=pltpu.SMEM)
HBM = pl.BlockSpec(memory_space=pltpu.HBM)
GRAM_CHUNK = 1152
TAIL_CHUNK = 1152
INNER = ((1,), (0,))
MIB = 2**20


def dot(left, right, dims=INNER, precision=None):
    return lax.dot_general(
        left, right, (dims, ((), ())), preferred_element_type=F32, precision=precision
    )


def split(x):
    high = x.astype(BF16)
    return high, (x - high.astype(F32)).astype(BF16)


def product(left, right, dims=INNER):
    return dot(left[0], right[0], dims) + (dot(left[1], right[0], dims) + dot(left[0], right[1], dims))


def halves(x, axis):
    return jnp.concatenate(split(x), axis=axis)


def folded(total):
    rows, columns = total.shape[0] // 2, total.shape[1] // 2
    top, bottom = total[:rows], total[rows:]
    return (top[:, :columns] + top[:, columns:]) + (bottom[:, :columns] + bottom[:, columns:])


def own_kernel(
    orb_hbm, app_hbm, cot_hbm, out_ref, cot_t_ref, orb, pair, sems
):
    cells = orb.shape[0]
    steps = cot_t_ref.shape[0]
    chunk = cells // steps
    copies = []
    for step in range(steps):
        rows = pl.ds(step * chunk, chunk)
        below = pl.ds(cells + step * chunk, chunk)
        group = [
            pltpu.make_async_copy(orb_hbm.at[rows], orb.at[rows], sems.at[step, 0]),
            pltpu.make_async_copy(cot_hbm.at[rows], pair.at[below], sems.at[step, 1]),
        ]
        for copy in group:
            copy.start()
        copies.append(group)
    last = pltpu.make_async_copy(app_hbm, pair.at[pl.ds(0, cells)], sems.at[steps, 0])
    last.start()
    total = None
    for step in range(steps):
        for copy in copies[step]:
            copy.wait()
        cot_t = halves(pair[pl.ds(cells + step * chunk, chunk), :].T, 0)
        cot_t_ref[step] = cot_t
        part = dot(cot_t, halves(orb[pl.ds(step * chunk, chunk), :], 1))
        total = part if total is None else total + part
    out_ref[...] = folded(total)
    last.wait()


def other_kernel(bcol_ref, own_ref, cot_t_ref, orb_ref, out_ref):
    steps = cot_t_ref.shape[0]
    chunk = orb_ref.shape[0] // steps
    width = own_ref.shape[0]
    total = None
    for step in range(steps):
        part = dot(cot_t_ref[step], halves(orb_ref[pl.ds(step * chunk, chunk), :], 1))
        total = part if total is None else total + part
    mine = bcol_ref[0]
    out_ref[pl.ds(pl.multiple_of(mine * width, width), width), :] = own_ref[...]
    out_ref[pl.ds(pl.multiple_of((1 - mine) * width, width), width), :] = folded(total)


def spread_kernel(parts_ref, panel_ref, out_ref):
    both = jnp.concatenate([jnp.sum(parts_ref[...], axis=0), panel_ref[...]], axis=0)
    out_ref[...] = jnp.broadcast_to(both[None], out_ref.shape)


def gather_kernel(parts_ref, out_ref, columns_ref):
    tile = out_ref.shape[1]
    out_ref[...] = jnp.broadcast_to(jnp.sum(parts_ref[:, :tile, :], axis=0)[None], out_ref.shape)
    columns_ref[...] = parts_ref[:, tile:, :].reshape(columns_ref.shape)


def join_kernel(sums_ref, columns_ref, out_ref):
    rows = sums_ref.shape[0]
    out_ref[:rows, :] = sums_ref[...]
    out_ref[rows:, :] = columns_ref[...]


def tail_kernel(
    bcol_ref, whole_ref, row_ref, orb, pair, orb_oth, pair_oth, out_hbm, result, weights, sems
):
    cells, width = result.shape
    steps = sems.shape[0]
    chunk = cells // steps
    mine = bcol_ref[0]
    bands = 2 * width
    first = pl.ds(pl.multiple_of(mine * width, width), width)
    second = pl.ds(pl.multiple_of((1 - mine) * width, width), width)
    grad_t = jnp.concatenate(
        [
            jnp.concatenate(
                [whole_ref[b * width : (b + 1) * width, c * width : (c + 1) * width] for b in range(2)],
                axis=1,
            )
            for c in range(2)
        ],
        axis=0,
    )
    rotation = split(whole_ref[bands:, :])
    gram_t = product(split(grad_t), rotation)
    at_row = lax.broadcasted_iota(jnp.int32, (bands, bands), 0)
    at_col = lax.broadcasted_iota(jnp.int32, (bands, bands), 1)
    diagonal = at_row == at_col
    levels_row = jnp.broadcast_to(row_ref[...], (bands, bands))
    levels_col = levels_row.T
    gaps = jnp.where(diagonal, 1.0, levels_col - levels_row)
    mixing_t = jnp.where(diagonal, 0.0, (1.0 / gaps) * gram_t)
    sym_ham = mixing_t + mixing_t.T
    scaled = levels_col * mixing_t
    sym_ovl = scaled + scaled.T + jnp.where(diagonal, gram_t, 0.0)
    rot_rows = whole_ref[pl.ds(pl.multiple_of(bands + mine * width, width), width), :]
    right = product(
        split(jnp.concatenate([sym_ovl, sym_ham], axis=0)), split(rot_rows), ((1,), (1,))
    )
    coefs = product(rotation, split(jnp.concatenate([-right[:bands], right[bands:]], axis=1)))
    for at, block in enumerate((coefs[:, :width], coefs[:, width:], rot_rows.T)):
        weights[at] = halves(block, 1)
    weight = jnp.concatenate(
        [weights[at, rows, :] for at in range(3) for rows in (first, second)], axis=0
    )
    outs = []
    for step in range(steps):
        rows = pl.ds(step * chunk, chunk)
        below = pl.ds(cells + step * chunk, chunk)
        left = jnp.concatenate(
            [
                orb[rows, :],
                orb_oth[rows, :],
                pair[rows, :],
                pair_oth[rows, :],
                pair[below, :],
                pair_oth[below, :],
            ],
            axis=1,
        )
        high, low = split(left)
        wide = dot(high, weight)
        result[rows, :] = wide[:, :width] + wide[:, width:] + dot(low, weight[:, :width])
        copy = pltpu.make_async_copy(result.at[rows], out_hbm.at[rows], sems.at[step])
        copy.start()
        outs.append(copy)
    for copy in outs:
        copy.wait()


def limit(mib):
    return pltpu.CompilerParams(vmem_limit_bytes=mib * MIB)


def own_gram(orbitals, applied, cotangent):
    cells, width = orbitals.shape
    steps = cells // GRAM_CHUNK
    return pl.pallas_call(
        own_kernel,
        out_shape=(
            jax.ShapeDtypeStruct((width, width), F32),
            jax.ShapeDtypeStruct((steps, 2 * width, GRAM_CHUNK), BF16),
            jax.ShapeDtypeStruct((cells, width), F32),
            jax.ShapeDtypeStruct((2 * cells, width), F32),
        ),
        in_specs=[HBM] * 3,
        out_specs=(VMEM,) * 4,
        scratch_shapes=[pltpu.SemaphoreType.DMA((steps + 1, 2))],
        compiler_params=limit(12),
        cost_estimate=pl.CostEstimate(
            flops=8 * cells * width * width, bytes_accessed=3 * 4 * cells * width, transcendentals=0
        ),
        name="own_gram",
    )(orbitals, applied, cotangent)


def whole_gram(mine, own, cot_t, orb_oth):
    cells, width = orb_oth.shape
    return pl.pallas_call(
        other_kernel,
        out_shape=jax.ShapeDtypeStruct((2 * width, width), F32),
        in_specs=[SMEM, VMEM, VMEM, VMEM],
        out_specs=VMEM,
        compiler_params=limit(10),
        name="whole_gram",
    )(mine, own, cot_t, orb_oth)


def spread(parts, panel, receivers):
    space, tile, width = parts.shape
    return pl.pallas_call(
        spread_kernel,
        out_shape=jax.ShapeDtypeStruct((receivers, tile + panel.shape[0], width), F32),
        in_specs=[VMEM, VMEM],
        out_specs=VMEM,
        compiler_params=limit(2),
        name="spread",
    )(parts, panel)


def gather(panels, space, tile):
    brow, rows, width = panels.shape
    return pl.pallas_call(
        gather_kernel,
        out_shape=(
            jax.ShapeDtypeStruct((space, tile, width), F32),
            jax.ShapeDtypeStruct((brow * (rows - tile), width), F32),
        ),
        in_specs=[VMEM],
        out_specs=(VMEM, VMEM),
        compiler_params=limit(2),
        name="gather",
    )(panels)


def join(sums, columns):
    rows, width = sums.shape
    return pl.pallas_call(
        join_kernel,
        out_shape=jax.ShapeDtypeStruct((2 * rows, width), F32),
        in_specs=[VMEM, VMEM],
        out_specs=VMEM,
        compiler_params=limit(2),
        name="join",
    )(sums, columns)


def tail(mine, whole, levels, orb, pair, orb_oth, pair_oth):
    cells, width = orb.shape
    bands = 2 * width
    steps = cells // TAIL_CHUNK
    return pl.pallas_call(
        tail_kernel,
        out_shape=jax.ShapeDtypeStruct((cells, width), F32),
        in_specs=[SMEM] + [VMEM] * 6,
        out_specs=HBM,
        scratch_shapes=[
            pltpu.VMEM((cells, width), F32),
            pltpu.VMEM((3, bands, bands), BF16),
            pltpu.SemaphoreType.DMA((steps,)),
        ],
        compiler_params=limit(20),
        name="tail",
    )(mine, whole, levels.reshape(1, bands), orb, pair, orb_oth, pair_oth)


def body(orbitals, applied, cotangent, panel, levels):
    width = orbitals.shape[1]
    swap = [(0, 1), (1, 0)]
    space = lax.axis_size("space")
    brow = lax.axis_size("brow")
    tile = 2 * width // space
    mine = lax.axis_index("bcol").reshape(1)

    blocks = [pltpu.with_memory_space_constraint(x, pltpu.HBM) for x in (orbitals, applied, cotangent)]
    orb_oth = lax.ppermute(orbitals, "bcol", swap)
    own, cot_t, orb, pair = own_gram(*blocks)
    partial = whole_gram(mine, own, cot_t, orb_oth)
    pair, partial = lax.optimization_barrier((pair, partial))
    pair_oth = lax.ppermute(pair, "bcol", swap)
    parts = lax.all_to_all(partial.reshape(space, tile, width), "space", 0, 0, tiled=True)
    panels = lax.all_to_all(spread(parts, panel, brow), "brow", 0, 0, tiled=True)
    tiles, columns = gather(panels, space, tile)
    sums = lax.all_to_all(tiles, "space", 0, 0, tiled=True).reshape(2 * width, width)
    whole = lax.all_gather(join(sums, columns), "bcol", axis=1, tiled=True)
    return tail(mine, whole, levels, orb, pair, orb_oth, pair_oth)


def solution(mesh):
    return jax.shard_map(
        body,
        mesh=mesh,
        in_specs=(
            P(("space", "brow"), "bcol"),
            P(("space", "brow"), "bcol"),
            P(("space", "brow"), "bcol"),
            P("brow", "bcol"),
            P(),
        ),
        out_specs=P(("space", "brow"), "bcol"),
        check_vma=False,
    )
```

```python
import jax
import jax.numpy as jnp
from jax import lax
from jax.experimental import pallas as pl
from jax.experimental.pallas import tpu as pltpu
from jax.sharding import Mesh
from jax.sharding import PartitionSpec as P

F32 = jnp.float32
BF16 = jnp.bfloat16
VMEM = pl.BlockSpec(memory_space=pltpu.VMEM)
HBM = pl.BlockSpec(memory_space=pltpu.HBM)
GRAM_CHUNK = 1152
TAIL_CHUNK = 1152
INNER = ((1,), (0,))
NEAR = ("zn", "x", "yn")
FAR = ("zf", "yf")
OCTET = 8
MIB = 2**20


def dot(left, right, dims=INNER, precision=None):
    return lax.dot_general(
        left, right, (dims, ((), ())), preferred_element_type=F32, precision=precision
    )


def split(x):
    high = x.astype(BF16)
    return high, (x - high.astype(F32)).astype(BF16)


def product(left, right, dims=INNER):
    return dot(left[0], right[0], dims) + (dot(left[1], right[0], dims) + dot(left[0], right[1], dims))


def halves(x, axis):
    return jnp.concatenate(split(x), axis=axis)


def folded(total):
    rows, columns = total.shape[0] // 2, total.shape[1] // 2
    top, bottom = total[:rows], total[rows:]
    return (top[:, :columns] + top[:, columns:]) + (bottom[:, :columns] + bottom[:, columns:])


def own_kernel(
    orb_hbm, app_hbm, cot_hbm, out_ref, cot_t_ref, orb, pair, sems
):
    cells = orb.shape[0]
    steps = cot_t_ref.shape[0]
    chunk = cells // steps
    copies = []
    for step in range(steps):
        rows = pl.ds(step * chunk, chunk)
        below = pl.ds(cells + step * chunk, chunk)
        group = [
            pltpu.make_async_copy(orb_hbm.at[rows], orb.at[rows], sems.at[step, 0]),
            pltpu.make_async_copy(cot_hbm.at[rows], pair.at[below], sems.at[step, 1]),
        ]
        for copy in group:
            copy.start()
        copies.append(group)
    last = pltpu.make_async_copy(app_hbm, pair.at[pl.ds(0, cells)], sems.at[steps, 0])
    last.start()
    total = None
    for step in range(steps):
        for copy in copies[step]:
            copy.wait()
        cot_t = halves(pair[pl.ds(cells + step * chunk, chunk), :].T, 0)
        cot_t_ref[step] = cot_t
        part = dot(cot_t, halves(orb[pl.ds(step * chunk, chunk), :], 1))
        total = part if total is None else total + part
    out_ref[...] = folded(total)
    last.wait()


def other_kernel(own_ref, cot_t_ref, orb_ref, out_ref):
    steps = cot_t_ref.shape[0]
    chunk = orb_ref.shape[0] // steps
    width = own_ref.shape[0]
    total = None
    for step in range(steps):
        part = dot(cot_t_ref[step], halves(orb_ref[pl.ds(step * chunk, chunk), :], 1))
        total = part if total is None else total + part
    mine = lax.axis_index("bcol")
    out_ref[pl.ds(pl.multiple_of(mine * width, width), width), :] = own_ref[...]
    out_ref[pl.ds(pl.multiple_of((1 - mine) * width, width), width), :] = folded(total)


def spread_kernel(parts_ref, panel_ref, out_ref):
    octet = pl.ds(pl.multiple_of(lax.axis_index("x") * OCTET, OCTET), OCTET)
    both = jnp.concatenate([jnp.sum(parts_ref[...], axis=0), panel_ref[octet, :]], axis=0)
    out_ref[...] = jnp.broadcast_to(both[None], out_ref.shape)


def gather_kernel(parts_ref, out_ref):
    tile = parts_ref.shape[1] - OCTET
    octets = parts_ref[pl.ds(2 * lax.axis_index("zn"), 2), tile:, :]
    total = jnp.sum(parts_ref[:, :tile, :], axis=0)
    both = jnp.concatenate([total, octets.reshape(2 * OCTET, total.shape[1])], axis=0)
    out_ref[...] = jnp.broadcast_to(both[None], out_ref.shape)


def tail_kernel(
    whole_ref, row_ref, orb, pair, orb_oth, pair_oth, out_hbm, result, weights, sems
):
    cells, width = result.shape
    steps = sems.shape[0]
    chunk = cells // steps
    mine = lax.axis_index("bcol")
    bands = 2 * width
    first = pl.ds(pl.multiple_of(mine * width, width), width)
    second = pl.ds(pl.multiple_of((1 - mine) * width, width), width)
    block = 4 * OCTET
    tile = 2 * OCTET
    sums = jnp.concatenate(
        [whole_ref[q * block : q * block + tile, :] for q in range(bands // tile)], axis=0
    )
    octets = []
    for y in range(bands // block):
        yf, yn = y // 2, y % 2
        for x in range(block // OCTET):
            at = (8 * (yf // 2) + 2 * x + yn) * block + tile + (yf % 2) * OCTET
            octets.append(whole_ref[at : at + OCTET, :])
    half = len(octets) // 2
    top, bottom = (jnp.concatenate(part, axis=0) for part in (octets[:half], octets[half:]))
    grad_t = jnp.concatenate(
        [
            jnp.concatenate(
                [sums[b * width : (b + 1) * width, c * width : (c + 1) * width] for b in range(2)],
                axis=1,
            )
            for c in range(2)
        ],
        axis=0,
    )
    rotation = split(jnp.concatenate([top, bottom], axis=0))
    rot_rows = jnp.where(mine == 0, top, bottom)
    gram_t = product(split(grad_t), rotation)
    at_row = lax.broadcasted_iota(jnp.int32, (bands, bands), 0)
    at_col = lax.broadcasted_iota(jnp.int32, (bands, bands), 1)
    diagonal = at_row == at_col
    levels_row = jnp.broadcast_to(row_ref[...], (bands, bands))
    levels_col = levels_row.T
    gaps = jnp.where(diagonal, 1.0, levels_col - levels_row)
    mixing_t = jnp.where(diagonal, 0.0, (1.0 / gaps) * gram_t)
    sym_ham = mixing_t + mixing_t.T
    scaled = levels_col * mixing_t
    sym_ovl = scaled + scaled.T + jnp.where(diagonal, gram_t, 0.0)
    right = product(
        split(jnp.concatenate([sym_ovl, sym_ham], axis=0)), split(rot_rows), ((1,), (1,))
    )
    coefs = product(rotation, split(jnp.concatenate([-right[:bands], right[bands:]], axis=1)))
    for at, block in enumerate((coefs[:, :width], coefs[:, width:], rot_rows.T)):
        weights[at] = halves(block, 1)
    weight = jnp.concatenate(
        [weights[at, rows, :] for at in range(3) for rows in (first, second)], axis=0
    )
    outs = []
    for step in range(steps):
        rows = pl.ds(step * chunk, chunk)
        below = pl.ds(cells + step * chunk, chunk)
        left = jnp.concatenate(
            [
                orb[rows, :],
                orb_oth[rows, :],
                pair[rows, :],
                pair_oth[rows, :],
                pair[below, :],
                pair_oth[below, :],
            ],
            axis=1,
        )
        high, low = split(left)
        wide = dot(high, weight)
        result[rows, :] = wide[:, :width] + wide[:, width:] + dot(low, weight[:, :width])
        copy = pltpu.make_async_copy(result.at[rows], out_hbm.at[rows], sems.at[step])
        copy.start()
        outs.append(copy)
    for copy in outs:
        copy.wait()


def limit(mib):
    return pltpu.CompilerParams(vmem_limit_bytes=mib * MIB)


def own_gram(orbitals, applied, cotangent):
    cells, width = orbitals.shape
    steps = cells // GRAM_CHUNK
    return pl.pallas_call(
        own_kernel,
        out_shape=(
            jax.ShapeDtypeStruct((width, width), F32),
            jax.ShapeDtypeStruct((steps, 2 * width, GRAM_CHUNK), BF16),
            jax.ShapeDtypeStruct((cells, width), F32),
            jax.ShapeDtypeStruct((2 * cells, width), F32),
        ),
        in_specs=[HBM] * 3,
        out_specs=(VMEM,) * 4,
        scratch_shapes=[pltpu.SemaphoreType.DMA((steps + 1, 2))],
        compiler_params=limit(12),
        cost_estimate=pl.CostEstimate(
            flops=8 * cells * width * width, bytes_accessed=3 * 4 * cells * width, transcendentals=0
        ),
        name="own_gram",
    )(orbitals, applied, cotangent)


def whole_gram(own, cot_t, orb_oth):
    cells, width = orb_oth.shape
    return pl.pallas_call(
        other_kernel,
        out_shape=jax.ShapeDtypeStruct((2 * width, width), F32),
        in_specs=[VMEM, VMEM, VMEM],
        out_specs=VMEM,
        compiler_params=limit(10),
        name="whole_gram",
    )(own, cot_t, orb_oth)


def spread(parts, panel, receivers):
    near, tile, width = parts.shape
    return pl.pallas_call(
        spread_kernel,
        out_shape=jax.ShapeDtypeStruct((receivers, tile + OCTET, width), F32),
        in_specs=[VMEM, VMEM],
        out_specs=VMEM,
        compiler_params=limit(2),
        name="spread",
    )(parts, panel)


def gather(parts, receivers):
    far, rows, width = parts.shape
    return pl.pallas_call(
        gather_kernel,
        out_shape=jax.ShapeDtypeStruct((receivers, rows + OCTET, width), F32),
        in_specs=[VMEM],
        out_specs=VMEM,
        compiler_params=limit(2),
        name="gather",
    )(parts)


def tail(whole, levels, orb, pair, orb_oth, pair_oth):
    cells, width = orb.shape
    bands = 2 * width
    steps = cells // TAIL_CHUNK
    return pl.pallas_call(
        tail_kernel,
        out_shape=jax.ShapeDtypeStruct((cells, width), F32),
        in_specs=[VMEM] * 6,
        out_specs=HBM,
        scratch_shapes=[
            pltpu.VMEM((cells, width), F32),
            pltpu.VMEM((3, bands, bands), BF16),
            pltpu.SemaphoreType.DMA((steps,)),
        ],
        compiler_params=limit(20),
        name="tail",
    )(whole, levels.reshape(1, bands), orb, pair, orb_oth, pair_oth)


def body(orbitals, applied, cotangent, panel, levels):
    width = orbitals.shape[1]
    swap = [(0, 1), (1, 0)]
    near = lax.axis_size(NEAR)
    far = lax.axis_size(FAR)

    blocks = [pltpu.with_memory_space_constraint(x, pltpu.HBM) for x in (orbitals, applied, cotangent)]
    orb_oth = lax.ppermute(orbitals, "bcol", swap)
    own, cot_t, orb, pair = own_gram(*blocks)
    partial = whole_gram(own, cot_t, orb_oth)
    pair, partial = lax.optimization_barrier((pair, partial))
    pair_oth = lax.ppermute(pair, "bcol", swap)
    parts = lax.all_to_all(partial.reshape(near, -1, width), NEAR, 0, 0, tiled=True)
    parts = lax.all_to_all(spread(parts, panel, far), FAR, 0, 0, tiled=True)
    sums = lax.all_to_all(gather(parts, near), NEAR, 0, 0, tiled=True)
    whole = lax.all_gather(sums.reshape(-1, width), "bcol", axis=1, tiled=True)
    return tail(whole, levels, orb, pair, orb_oth, pair_oth)


def solution(mesh):
    fine = Mesh(mesh.devices.reshape(4, 2, 4, 4, 2, 2), ("zf", "zn", "x", "yf", "yn", "bcol"))
    cells = P(("zf", "zn", "x", "yf", "yn"), "bcol")
    return jax.shard_map(
        body,
        mesh=fine,
        in_specs=(cells, cells, cells, P(("yf", "yn"), "bcol"), P()),
        out_specs=cells,
        check_vma=False,
    )
```

```python
import jax
import jax.numpy as jnp
from jax import lax
from jax.experimental import pallas as pl
from jax.experimental.pallas import tpu as pltpu
from jax.sharding import Mesh
from jax.sharding import PartitionSpec as P

F32 = jnp.float32
BF16 = jnp.bfloat16
VMEM = pl.BlockSpec(memory_space=pltpu.VMEM)
HBM = pl.BlockSpec(memory_space=pltpu.HBM)
GRAM_CHUNK = 1152
TAIL_CHUNK = 576
INNER = ((1,), (0,))
NEAR = ("zn", "x", "yn")
FAR = ("zf", "yf")
OCTET = 8
MIB = 2**20


def dot(left, right, dims=INNER, precision=None):
    return lax.dot_general(
        left, right, (dims, ((), ())), preferred_element_type=F32, precision=precision
    )


def split(x):
    high = x.astype(BF16)
    return high, (x - high.astype(F32)).astype(BF16)


def product(left, right, dims=INNER):
    return dot(left[0], right[0], dims) + (dot(left[1], right[0], dims) + dot(left[0], right[1], dims))


def halves(x, axis):
    return jnp.concatenate(split(x), axis=axis)


def folded(total):
    rows, columns = total.shape[0] // 2, total.shape[1] // 2
    top, bottom = total[:rows], total[rows:]
    return (top[:, :columns] + top[:, columns:]) + (bottom[:, :columns] + bottom[:, columns:])


def own_kernel(
    orb_hbm, app_hbm, cot_hbm, out_ref, cot_t_ref, orb, pair, sems
):
    cells = orb.shape[0]
    steps = cot_t_ref.shape[0]
    chunk = cells // steps
    copies = []
    for step in range(steps):
        rows = pl.ds(step * chunk, chunk)
        below = pl.ds(cells + step * chunk, chunk)
        group = [
            pltpu.make_async_copy(orb_hbm.at[rows], orb.at[rows], sems.at[step, 0]),
            pltpu.make_async_copy(cot_hbm.at[rows], pair.at[below], sems.at[step, 1]),
        ]
        for copy in group:
            copy.start()
        copies.append(group)
    last = pltpu.make_async_copy(app_hbm, pair.at[pl.ds(0, cells)], sems.at[steps, 0])
    last.start()
    total = None
    for step in range(steps):
        for copy in copies[step]:
            copy.wait()
        cot_t = halves(pair[pl.ds(cells + step * chunk, chunk), :].T, 0)
        cot_t_ref[step] = cot_t
        part = dot(cot_t, halves(orb[pl.ds(step * chunk, chunk), :], 1))
        total = part if total is None else total + part
    out_ref[...] = folded(total)
    last.wait()


def other_kernel(own_ref, cot_t_ref, orb_ref, out_ref):
    steps = cot_t_ref.shape[0]
    chunk = orb_ref.shape[0] // steps
    width = own_ref.shape[0]
    total = None
    for step in range(steps):
        part = dot(cot_t_ref[step], halves(orb_ref[pl.ds(step * chunk, chunk), :], 1))
        total = part if total is None else total + part
    mine = lax.axis_index("bcol")
    out_ref[pl.ds(pl.multiple_of(mine * width, width), width), :] = own_ref[...]
    out_ref[pl.ds(pl.multiple_of((1 - mine) * width, width), width), :] = folded(total)


def spread_kernel(parts_ref, panel_ref, out_ref):
    octet = pl.ds(pl.multiple_of(lax.axis_index("x") * OCTET, OCTET), OCTET)
    both = jnp.concatenate([jnp.sum(parts_ref[...], axis=0), panel_ref[octet, :]], axis=0)
    out_ref[...] = jnp.broadcast_to(both[None], out_ref.shape)


def gather_kernel(parts_ref, out_ref):
    tile = parts_ref.shape[1] - OCTET
    octets = parts_ref[pl.ds(2 * lax.axis_index("zn"), 2), tile:, :]
    total = jnp.sum(parts_ref[:, :tile, :], axis=0)
    both = jnp.concatenate([total, octets.reshape(2 * OCTET, total.shape[1])], axis=0)
    out_ref[...] = jnp.broadcast_to(both[None], out_ref.shape)


def tail_kernel(
    whole_ref, row_ref, orb, pair, orb_oth, pair_oth, out_hbm, result, weights, sems
):
    cells, width = result.shape
    steps = sems.shape[0]
    chunk = cells // steps
    mine = lax.axis_index("bcol")
    bands = 2 * width
    first = pl.ds(pl.multiple_of(mine * width, width), width)
    second = pl.ds(pl.multiple_of((1 - mine) * width, width), width)
    block = 4 * OCTET
    tile = 2 * OCTET
    sums = jnp.concatenate(
        [whole_ref[q * block : q * block + tile, :] for q in range(bands // tile)], axis=0
    )
    octets = []
    for y in range(bands // block):
        yf, yn = y // 2, y % 2
        for x in range(block // OCTET):
            at = (8 * (yf // 2) + 2 * x + yn) * block + tile + (yf % 2) * OCTET
            octets.append(whole_ref[at : at + OCTET, :])
    half = len(octets) // 2
    top, bottom = (jnp.concatenate(part, axis=0) for part in (octets[:half], octets[half:]))
    grad_t = jnp.concatenate(
        [
            jnp.concatenate(
                [sums[b * width : (b + 1) * width, c * width : (c + 1) * width] for b in range(2)],
                axis=1,
            )
            for c in range(2)
        ],
        axis=0,
    )
    rotation = split(jnp.concatenate([top, bottom], axis=0))
    rot_rows = jnp.where(mine == 0, top, bottom)
    weights[2] = halves(rot_rows.T, 1)
    weight = jnp.concatenate([weights[2, first, :], weights[2, second, :]], axis=0)

    def rotated(step):
        below = pl.ds(cells + step * chunk, chunk)
        high, low = split(jnp.concatenate([pair[below, :], pair_oth[below, :]], axis=1))
        wide = dot(high, weight)
        rows = pl.ds(step * chunk, chunk)
        result[rows, :] = wide[:, :width] + wide[:, width:] + dot(low, weight[:, :width])

    gram_t = product(split(grad_t), rotation)
    rotated(0)
    at_row = lax.broadcasted_iota(jnp.int32, (bands, bands), 0)
    at_col = lax.broadcasted_iota(jnp.int32, (bands, bands), 1)
    diagonal = at_row == at_col
    levels_row = jnp.broadcast_to(row_ref[...], (bands, bands))
    levels_col = levels_row.T
    gaps = jnp.where(diagonal, 1.0, levels_col - levels_row)
    mixing_t = jnp.where(diagonal, 0.0, (1.0 / gaps) * gram_t)
    sym_ham = mixing_t + mixing_t.T
    scaled = levels_col * mixing_t
    sym_ovl = scaled + scaled.T + jnp.where(diagonal, gram_t, 0.0)
    right = product(
        split(jnp.concatenate([sym_ovl, sym_ham], axis=0)), split(rot_rows), ((1,), (1,))
    )
    rotated(1)
    coefs = product(rotation, split(jnp.concatenate([-right[:bands], right[bands:]], axis=1)))
    for step in range(2, steps):
        rotated(step)
    for at, block in enumerate((coefs[:, :width], coefs[:, width:])):
        weights[at] = halves(block, 1)
    weight = jnp.concatenate(
        [weights[at, rows, :] for at in range(2) for rows in (first, second)], axis=0
    )
    outs = []
    for step in range(steps):
        rows = pl.ds(step * chunk, chunk)
        left = jnp.concatenate(
            [orb[rows, :], orb_oth[rows, :], pair[rows, :], pair_oth[rows, :]], axis=1
        )
        high, low = split(left)
        wide = dot(high, weight)
        result[rows, :] += wide[:, :width] + wide[:, width:] + dot(low, weight[:, :width])
        copy = pltpu.make_async_copy(result.at[rows], out_hbm.at[rows], sems.at[step])
        copy.start()
        outs.append(copy)
    for copy in outs:
        copy.wait()


def limit(mib):
    return pltpu.CompilerParams(vmem_limit_bytes=mib * MIB)


def own_gram(orbitals, applied, cotangent):
    cells, width = orbitals.shape
    steps = cells // GRAM_CHUNK
    return pl.pallas_call(
        own_kernel,
        out_shape=(
            jax.ShapeDtypeStruct((width, width), F32),
            jax.ShapeDtypeStruct((steps, 2 * width, GRAM_CHUNK), BF16),
            jax.ShapeDtypeStruct((cells, width), F32),
            jax.ShapeDtypeStruct((2 * cells, width), F32),
        ),
        in_specs=[HBM] * 3,
        out_specs=(VMEM,) * 4,
        scratch_shapes=[pltpu.SemaphoreType.DMA((steps + 1, 2))],
        compiler_params=limit(12),
        cost_estimate=pl.CostEstimate(
            flops=8 * cells * width * width, bytes_accessed=3 * 4 * cells * width, transcendentals=0
        ),
        name="own_gram",
    )(orbitals, applied, cotangent)


def whole_gram(own, cot_t, orb_oth):
    cells, width = orb_oth.shape
    return pl.pallas_call(
        other_kernel,
        out_shape=jax.ShapeDtypeStruct((2 * width, width), F32),
        in_specs=[VMEM, VMEM, VMEM],
        out_specs=VMEM,
        compiler_params=limit(10),
        name="whole_gram",
    )(own, cot_t, orb_oth)


def spread(parts, panel, receivers):
    near, tile, width = parts.shape
    return pl.pallas_call(
        spread_kernel,
        out_shape=jax.ShapeDtypeStruct((receivers, tile + OCTET, width), F32),
        in_specs=[VMEM, VMEM],
        out_specs=VMEM,
        compiler_params=limit(2),
        name="spread",
    )(parts, panel)


def gather(parts, receivers):
    far, rows, width = parts.shape
    return pl.pallas_call(
        gather_kernel,
        out_shape=jax.ShapeDtypeStruct((receivers, rows + OCTET, width), F32),
        in_specs=[VMEM],
        out_specs=VMEM,
        compiler_params=limit(2),
        name="gather",
    )(parts)


def tail(whole, levels, orb, pair, orb_oth, pair_oth):
    cells, width = orb.shape
    bands = 2 * width
    steps = cells // TAIL_CHUNK
    return pl.pallas_call(
        tail_kernel,
        out_shape=jax.ShapeDtypeStruct((cells, width), F32),
        in_specs=[VMEM] * 6,
        out_specs=HBM,
        scratch_shapes=[
            pltpu.VMEM((cells, width), F32),
            pltpu.VMEM((3, bands, bands), BF16),
            pltpu.SemaphoreType.DMA((steps,)),
        ],
        compiler_params=limit(20),
        name="tail",
    )(whole, levels.reshape(1, bands), orb, pair, orb_oth, pair_oth)


def body(orbitals, applied, cotangent, panel, levels):
    width = orbitals.shape[1]
    swap = [(0, 1), (1, 0)]
    near = lax.axis_size(NEAR)
    far = lax.axis_size(FAR)

    blocks = [pltpu.with_memory_space_constraint(x, pltpu.HBM) for x in (orbitals, applied, cotangent)]
    orb_oth = lax.ppermute(orbitals, "bcol", swap)
    own, cot_t, orb, pair = own_gram(*blocks)
    pair, own, cot_t = lax.optimization_barrier((pair, own, cot_t))
    pair_oth = lax.ppermute(pair, "bcol", swap)
    partial = whole_gram(own, cot_t, orb_oth)
    parts = lax.all_to_all(partial.reshape(near, -1, width), NEAR, 0, 0, tiled=True)
    parts = lax.all_to_all(spread(parts, panel, far), FAR, 0, 0, tiled=True)
    sums = lax.all_to_all(gather(parts, near), NEAR, 0, 0, tiled=True)
    whole = lax.all_gather(sums.reshape(-1, width), "bcol", axis=1, tiled=True)
    return tail(whole, levels, orb, pair, orb_oth, pair_oth)


def solution(mesh):
    fine = Mesh(mesh.devices.reshape(4, 2, 4, 4, 2, 2), ("zf", "zn", "x", "yf", "yn", "bcol"))
    cells = P(("zf", "zn", "x", "yf", "yn"), "bcol")
    return jax.shard_map(
        body,
        mesh=fine,
        in_specs=(cells, cells, cells, P(("yf", "yn"), "bcol"), P()),
        out_specs=cells,
        check_vma=False,
    )
```

```python
import itertools

import jax
import jax.numpy as jnp
from jax import lax
from jax.experimental import pallas as pl
from jax.experimental.pallas import tpu as pltpu
from jax.sharding import Mesh
from jax.sharding import PartitionSpec as P

F32 = jnp.float32
BF16 = jnp.bfloat16
VMEM = pl.BlockSpec(memory_space=pltpu.VMEM)
HBM = pl.BlockSpec(memory_space=pltpu.HBM)
GRAM_CHUNK = 1152
TAIL_CHUNK = 576
INNER = ((1,), (0,))
NEAR = ("zn", "x", "yn")
CELLS = ("zf", "zn", "x", "yf", "yn")
OCTET = 8
MIB = 2**20


def dot(left, right, dims=INNER, precision=None):
    return lax.dot_general(
        left, right, (dims, ((), ())), preferred_element_type=F32, precision=precision
    )


def mirrored(block, near):
    return 2 * block + (near + block // 2) % 2


def far_groups():
    return [
        [
            mirrored(zf, zn) * 32 + x * 8 + mirrored(yf, yn)
            for zf, yf in itertools.product(range(4), range(4))
        ]
        for zn, x, yn in itertools.product(range(2), range(4), range(2))
    ]


def flips():
    return lax.axis_index("zf") // 2, lax.axis_index("yf") // 2


def place(tile, z_flip, y_flip):
    zn, x, yn = tile // 8, tile // 2 % 4, tile % 2
    z = 1 - z_flip if zn else z_flip
    y = 1 - y_flip if yn else y_flip
    return 8 * z + 2 * x + y


def split(x):
    high = x.astype(BF16)
    return high, (x - high.astype(F32)).astype(BF16)


def product(left, right, dims=INNER):
    return dot(left[0], right[0], dims) + (dot(left[1], right[0], dims) + dot(left[0], right[1], dims))


def halves(x, axis):
    return jnp.concatenate(split(x), axis=axis)


def folded(total):
    rows, columns = total.shape[0] // 2, total.shape[1] // 2
    top, bottom = total[:rows], total[rows:]
    return (top[:, :columns] + top[:, columns:]) + (bottom[:, :columns] + bottom[:, columns:])


def own_kernel(
    orb_hbm, app_hbm, cot_hbm, out_ref, cot_t_ref, orb, pair, sems
):
    cells = orb.shape[0]
    steps = cot_t_ref.shape[0]
    chunk = cells // steps
    copies = []
    for step in range(steps):
        rows = pl.ds(step * chunk, chunk)
        below = pl.ds(cells + step * chunk, chunk)
        group = [
            pltpu.make_async_copy(orb_hbm.at[rows], orb.at[rows], sems.at[step, 0]),
            pltpu.make_async_copy(cot_hbm.at[rows], pair.at[below], sems.at[step, 1]),
        ]
        for copy in group:
            copy.start()
        copies.append(group)
    last = pltpu.make_async_copy(app_hbm, pair.at[pl.ds(0, cells)], sems.at[steps, 0])
    last.start()
    total = None
    for step in range(steps):
        for copy in copies[step]:
            copy.wait()
        cot_t = halves(pair[pl.ds(cells + step * chunk, chunk), :].T, 0)
        cot_t_ref[step] = cot_t
        part = dot(cot_t, halves(orb[pl.ds(step * chunk, chunk), :], 1))
        total = part if total is None else total + part
    out_ref[...] = folded(total)
    last.wait()


def other_kernel(own_ref, cot_t_ref, orb_ref, out_ref):
    steps = cot_t_ref.shape[0]
    chunk = orb_ref.shape[0] // steps
    width = own_ref.shape[0]
    total = None
    for step in range(steps):
        part = dot(cot_t_ref[step], halves(orb_ref[pl.ds(step * chunk, chunk), :], 1))
        total = part if total is None else total + part
    other = folded(total)
    first = lax.axis_index("bcol") == 0
    parts = (jnp.where(first, own_ref[...], other), jnp.where(first, other, own_ref[...]))
    rows = jnp.concatenate(parts, axis=0)
    turned = flips()
    tile = out_ref.shape[1]
    for at in range(out_ref.shape[0]):
        out_ref[place(at, *turned)] = rows[at * tile : (at + 1) * tile, :]


def spread_kernel(parts_ref, panel_ref, out_ref):
    octet = pl.ds(pl.multiple_of(lax.axis_index("x") * OCTET, OCTET), OCTET)
    both = jnp.concatenate([jnp.sum(parts_ref[...], axis=0), panel_ref[octet, :]], axis=0)
    out_ref[...] = jnp.broadcast_to(both[None], out_ref.shape)


def gather_kernel(parts_ref, out_ref):
    tile = parts_ref.shape[1] - OCTET
    zn = (lax.axis_index("zn") + flips()[0]) % 2
    octets = parts_ref[pl.ds(2 * zn, 2), tile:, :]
    total = jnp.sum(parts_ref[:, :tile, :], axis=0)
    both = jnp.concatenate([total, octets.reshape(2 * OCTET, total.shape[1])], axis=0)
    out_ref[...] = jnp.broadcast_to(both[None], out_ref.shape)


def tail_kernel(
    whole_ref, row_ref, orb, pair, orb_oth, pair_oth, out_hbm, result, weights, sems
):
    cells, width = result.shape
    steps = sems.shape[0]
    chunk = cells // steps
    mine = lax.axis_index("bcol")
    bands = 2 * width
    first = pl.ds(pl.multiple_of(mine * width, width), width)
    second = pl.ds(pl.multiple_of((1 - mine) * width, width), width)
    block = 4 * OCTET
    tile = 2 * OCTET
    turned = flips()
    starts = [pl.multiple_of(place(at, *turned) * block, block) for at in range(bands // tile)]
    sums = jnp.concatenate([whole_ref[pl.ds(start, tile), :] for start in starts], axis=0)
    octets = []
    for y in range(bands // block):
        zn, slot = y // 4, y // 2 % 2
        yn = (y + zn) % 2
        for x in range(block // OCTET):
            start = starts[8 * zn + 2 * x + yn] + (tile + slot * OCTET)
            octets.append(whole_ref[pl.ds(pl.multiple_of(start, OCTET), OCTET), :])
    half = len(octets) // 2
    top, bottom = (jnp.concatenate(part, axis=0) for part in (octets[:half], octets[half:]))
    grad_t = jnp.concatenate(
        [
            jnp.concatenate(
                [sums[b * width : (b + 1) * width, c * width : (c + 1) * width] for b in range(2)],
                axis=1,
            )
            for c in range(2)
        ],
        axis=0,
    )
    rotation = split(jnp.concatenate([top, bottom], axis=0))
    rot_rows = jnp.where(mine == 0, top, bottom)
    weights[2] = halves(rot_rows.T, 1)
    weight = jnp.concatenate([weights[2, first, :], weights[2, second, :]], axis=0)

    def rotated(step):
        below = pl.ds(cells + step * chunk, chunk)
        high, low = split(jnp.concatenate([pair[below, :], pair_oth[below, :]], axis=1))
        wide = dot(high, weight)
        rows = pl.ds(step * chunk, chunk)
        result[rows, :] = wide[:, :width] + wide[:, width:] + dot(low, weight[:, :width])

    gram_t = product(split(grad_t), rotation)
    rotated(0)
    at_row = lax.broadcasted_iota(jnp.int32, (bands, bands), 0)
    at_col = lax.broadcasted_iota(jnp.int32, (bands, bands), 1)
    diagonal = at_row == at_col
    levels_row = jnp.broadcast_to(row_ref[...], (bands, bands))
    levels_col = levels_row.T
    gaps = jnp.where(diagonal, 1.0, levels_col - levels_row)
    mixing_t = jnp.where(diagonal, 0.0, (1.0 / gaps) * gram_t)
    sym_ham = mixing_t + mixing_t.T
    scaled = levels_col * mixing_t
    sym_ovl = scaled + scaled.T + jnp.where(diagonal, gram_t, 0.0)
    right = product(
        split(jnp.concatenate([sym_ovl, sym_ham], axis=0)), split(rot_rows), ((1,), (1,))
    )
    rotated(1)
    coefs = product(rotation, split(jnp.concatenate([-right[:bands], right[bands:]], axis=1)))
    for step in range(2, steps):
        rotated(step)
    for at, block in enumerate((coefs[:, :width], coefs[:, width:])):
        weights[at] = halves(block, 1)
    weight = jnp.concatenate(
        [weights[at, rows, :] for at in range(2) for rows in (first, second)], axis=0
    )
    outs = []
    for step in range(steps):
        rows = pl.ds(step * chunk, chunk)
        left = jnp.concatenate(
            [orb[rows, :], orb_oth[rows, :], pair[rows, :], pair_oth[rows, :]], axis=1
        )
        high, low = split(left)
        wide = dot(high, weight)
        result[rows, :] += wide[:, :width] + wide[:, width:] + dot(low, weight[:, :width])
        copy = pltpu.make_async_copy(result.at[rows], out_hbm.at[rows], sems.at[step])
        copy.start()
        outs.append(copy)
    for copy in outs:
        copy.wait()


def limit(mib):
    return pltpu.CompilerParams(vmem_limit_bytes=mib * MIB)


def own_gram(orbitals, applied, cotangent):
    cells, width = orbitals.shape
    steps = cells // GRAM_CHUNK
    return pl.pallas_call(
        own_kernel,
        out_shape=(
            jax.ShapeDtypeStruct((width, width), F32),
            jax.ShapeDtypeStruct((steps, 2 * width, GRAM_CHUNK), BF16),
            jax.ShapeDtypeStruct((cells, width), F32),
            jax.ShapeDtypeStruct((2 * cells, width), F32),
        ),
        in_specs=[HBM] * 3,
        out_specs=(VMEM,) * 4,
        scratch_shapes=[pltpu.SemaphoreType.DMA((steps + 1, 2))],
        compiler_params=limit(12),
        cost_estimate=pl.CostEstimate(
            flops=8 * cells * width * width, bytes_accessed=3 * 4 * cells * width, transcendentals=0
        ),
        name="own_gram",
    )(orbitals, applied, cotangent)


def whole_gram(own, cot_t, orb_oth, near):
    cells, width = orb_oth.shape
    return pl.pallas_call(
        other_kernel,
        out_shape=jax.ShapeDtypeStruct((near, 2 * width // near, width), F32),
        in_specs=[VMEM, VMEM, VMEM],
        out_specs=VMEM,
        compiler_params=limit(10),
        name="whole_gram",
    )(own, cot_t, orb_oth)


def spread(parts, panel, receivers):
    near, tile, width = parts.shape
    return pl.pallas_call(
        spread_kernel,
        out_shape=jax.ShapeDtypeStruct((receivers, tile + OCTET, width), F32),
        in_specs=[VMEM, VMEM],
        out_specs=VMEM,
        compiler_params=limit(2),
        name="spread",
    )(parts, panel)


def gather(parts, receivers):
    far, rows, width = parts.shape
    return pl.pallas_call(
        gather_kernel,
        out_shape=jax.ShapeDtypeStruct((receivers, rows + OCTET, width), F32),
        in_specs=[VMEM],
        out_specs=VMEM,
        compiler_params=limit(2),
        name="gather",
    )(parts)


def tail(whole, levels, orb, pair, orb_oth, pair_oth):
    cells, width = orb.shape
    bands = 2 * width
    steps = cells // TAIL_CHUNK
    return pl.pallas_call(
        tail_kernel,
        out_shape=jax.ShapeDtypeStruct((cells, width), F32),
        in_specs=[VMEM] * 6,
        out_specs=HBM,
        scratch_shapes=[
            pltpu.VMEM((cells, width), F32),
            pltpu.VMEM((3, bands, bands), BF16),
            pltpu.SemaphoreType.DMA((steps,)),
        ],
        compiler_params=limit(20),
        name="tail",
    )(whole, levels.reshape(1, bands), orb, pair, orb_oth, pair_oth)


def body(orbitals, applied, cotangent, panel, levels):
    width = orbitals.shape[1]
    swap = [(0, 1), (1, 0)]
    near = lax.axis_size(NEAR)
    groups = far_groups()
    far = len(groups[0])

    blocks = [pltpu.with_memory_space_constraint(x, pltpu.HBM) for x in (orbitals, applied, cotangent)]
    orb_oth = lax.ppermute(orbitals, "bcol", swap)
    own, cot_t, orb, pair = own_gram(*blocks)
    pair, own, cot_t = lax.optimization_barrier((pair, own, cot_t))
    pair_oth = lax.ppermute(pair, "bcol", swap)
    partial = whole_gram(own, cot_t, orb_oth, near)
    parts = lax.all_to_all(partial, NEAR, 0, 0, tiled=True)
    parts = lax.all_to_all(
        spread(parts, panel, far), CELLS, 0, 0, tiled=True, axis_index_groups=groups
    )
    sums = lax.all_to_all(gather(parts, near), NEAR, 0, 0, tiled=True)
    whole = lax.all_gather(sums.reshape(-1, width), "bcol", axis=1, tiled=True)
    return tail(whole, levels, orb, pair, orb_oth, pair_oth)


def solution(mesh):
    fine = Mesh(mesh.devices.reshape(4, 2, 4, 4, 2, 2), ("zf", "zn", "x", "yf", "yn", "bcol"))
    cells = P(CELLS, "bcol")
    return jax.shard_map(
        body,
        mesh=fine,
        in_specs=(cells, cells, cells, P(("yf", "yn"), "bcol"), P()),
        out_specs=cells,
        check_vma=False,
    )
```

```python
import itertools

import jax
import jax.numpy as jnp
from jax import lax
from jax.experimental import pallas as pl
from jax.experimental.pallas import tpu as pltpu
from jax.sharding import Mesh
from jax.sharding import PartitionSpec as P

F32 = jnp.float32
BF16 = jnp.bfloat16
VMEM = pl.BlockSpec(memory_space=pltpu.VMEM)
HBM = pl.BlockSpec(memory_space=pltpu.HBM)
GRAM_CHUNK = 1152
TAIL_CHUNK = 576
INNER = ((1,), (0,))
NEAR = ("zn", "x", "yn")
CELLS = ("zf", "zn", "x", "yf", "yn")
OCTET = 8
MIB = 2**20


def dot(left, right, dims=INNER, precision=None):
    return lax.dot_general(
        left, right, (dims, ((), ())), preferred_element_type=F32, precision=precision
    )


def far_groups():
    return [
        [
            (2 * zf + zn) * 32 + x * 8 + 2 * yf + (yn + yf // 2) % 2
            for zf, yf in itertools.product(range(4), range(4))
        ]
        for zn, x, yn in itertools.product(range(2), range(4), range(2))
    ]


def upper():
    return lax.axis_index("yf") // 2


def place(tile, mirror):
    return tile - mirror if tile % 2 else tile + mirror


def split(x):
    high = x.astype(BF16)
    return high, (x - high.astype(F32)).astype(BF16)


def product(left, right, dims=INNER):
    return dot(left[0], right[0], dims) + (dot(left[1], right[0], dims) + dot(left[0], right[1], dims))


def halves(x, axis):
    return jnp.concatenate(split(x), axis=axis)


def folded(total):
    rows, columns = total.shape[0] // 2, total.shape[1] // 2
    top, bottom = total[:rows], total[rows:]
    return (top[:, :columns] + top[:, columns:]) + (bottom[:, :columns] + bottom[:, columns:])


def own_kernel(
    orb_hbm, app_hbm, cot_hbm, out_ref, cot_t_ref, orb, pair, sems
):
    cells = orb.shape[0]
    steps = cot_t_ref.shape[0]
    chunk = cells // steps
    copies = []
    for step in range(steps):
        rows = pl.ds(step * chunk, chunk)
        below = pl.ds(cells + step * chunk, chunk)
        group = [
            pltpu.make_async_copy(orb_hbm.at[rows], orb.at[rows], sems.at[step, 0]),
            pltpu.make_async_copy(cot_hbm.at[rows], pair.at[below], sems.at[step, 1]),
        ]
        for copy in group:
            copy.start()
        copies.append(group)
    last = pltpu.make_async_copy(app_hbm, pair.at[pl.ds(0, cells)], sems.at[steps, 0])
    last.start()
    total = None
    for step in range(steps):
        for copy in copies[step]:
            copy.wait()
        cot_t = halves(pair[pl.ds(cells + step * chunk, chunk), :].T, 0)
        cot_t_ref[step] = cot_t
        part = dot(cot_t, halves(orb[pl.ds(step * chunk, chunk), :], 1))
        total = part if total is None else total + part
    out_ref[...] = folded(total)
    last.wait()


def other_kernel(own_ref, cot_t_ref, orb_ref, out_ref):
    steps = cot_t_ref.shape[0]
    chunk = orb_ref.shape[0] // steps
    width = own_ref.shape[0]
    total = None
    for step in range(steps):
        part = dot(cot_t_ref[step], halves(orb_ref[pl.ds(step * chunk, chunk), :], 1))
        total = part if total is None else total + part
    other = folded(total)
    first = lax.axis_index("bcol") == 0
    parts = (jnp.where(first, own_ref[...], other), jnp.where(first, other, own_ref[...]))
    rows = jnp.concatenate(parts, axis=0)
    mirror = upper()
    tile = out_ref.shape[1]
    for at in range(out_ref.shape[0]):
        out_ref[place(at, mirror)] = rows[at * tile : (at + 1) * tile, :]


def spread_kernel(parts_ref, panel_ref, out_ref):
    octet = pl.ds(pl.multiple_of(lax.axis_index("x") * OCTET, OCTET), OCTET)
    both = jnp.concatenate([jnp.sum(parts_ref[...], axis=0), panel_ref[octet, :]], axis=0)
    out_ref[...] = jnp.broadcast_to(both[None], out_ref.shape)


def gather_kernel(parts_ref, out_ref):
    tile = parts_ref.shape[1] - OCTET
    octets = parts_ref[pl.ds(2 * lax.axis_index("zn"), 2), tile:, :]
    total = jnp.sum(parts_ref[:, :tile, :], axis=0)
    both = jnp.concatenate([total, octets.reshape(2 * OCTET, total.shape[1])], axis=0)
    out_ref[...] = jnp.broadcast_to(both[None], out_ref.shape)


def tail_kernel(
    whole_ref, row_ref, orb, pair, orb_oth, pair_oth, out_hbm, result, weights, sems
):
    cells, width = result.shape
    steps = sems.shape[0]
    chunk = cells // steps
    mine = lax.axis_index("bcol")
    bands = 2 * width
    first = pl.ds(pl.multiple_of(mine * width, width), width)
    second = pl.ds(pl.multiple_of((1 - mine) * width, width), width)
    block = 4 * OCTET
    tile = 2 * OCTET
    mirror = upper()
    starts = [pl.multiple_of(place(at, mirror) * block, block) for at in range(bands // tile)]
    sums = jnp.concatenate([whole_ref[pl.ds(start, tile), :] for start in starts], axis=0)
    octets = []
    for y in range(bands // block):
        zn, slot = y // 4, y // 2 % 2
        yn = (y + zn) % 2
        for x in range(block // OCTET):
            start = starts[8 * zn + 2 * x + yn] + (tile + slot * OCTET)
            octets.append(whole_ref[pl.ds(pl.multiple_of(start, OCTET), OCTET), :])
    half = len(octets) // 2
    top, bottom = (jnp.concatenate(part, axis=0) for part in (octets[:half], octets[half:]))
    grad_t = jnp.concatenate(
        [
            jnp.concatenate(
                [sums[b * width : (b + 1) * width, c * width : (c + 1) * width] for b in range(2)],
                axis=1,
            )
            for c in range(2)
        ],
        axis=0,
    )
    rotation = split(jnp.concatenate([top, bottom], axis=0))
    rot_rows = jnp.where(mine == 0, top, bottom)
    weights[2] = halves(rot_rows.T, 1)
    weight = jnp.concatenate([weights[2, first, :], weights[2, second, :]], axis=0)

    def rotated(step):
        below = pl.ds(cells + step * chunk, chunk)
        high, low = split(jnp.concatenate([pair[below, :], pair_oth[below, :]], axis=1))
        wide = dot(high, weight)
        rows = pl.ds(step * chunk, chunk)
        result[rows, :] = wide[:, :width] + wide[:, width:] + dot(low, weight[:, :width])

    gram_t = product(split(grad_t), rotation)
    rotated(0)
    at_row = lax.broadcasted_iota(jnp.int32, (bands, bands), 0)
    at_col = lax.broadcasted_iota(jnp.int32, (bands, bands), 1)
    diagonal = at_row == at_col
    levels_row = jnp.broadcast_to(row_ref[...], (bands, bands))
    levels_col = levels_row.T
    gaps = jnp.where(diagonal, 1.0, levels_col - levels_row)
    mixing_t = jnp.where(diagonal, 0.0, (1.0 / gaps) * gram_t)
    sym_ham = mixing_t + mixing_t.T
    scaled = levels_col * mixing_t
    sym_ovl = scaled + scaled.T + jnp.where(diagonal, gram_t, 0.0)
    right = product(
        split(jnp.concatenate([sym_ovl, sym_ham], axis=0)), split(rot_rows), ((1,), (1,))
    )
    rotated(1)
    coefs = product(rotation, split(jnp.concatenate([-right[:bands], right[bands:]], axis=1)))
    for step in range(2, steps):
        rotated(step)
    for at, block in enumerate((coefs[:, :width], coefs[:, width:])):
        weights[at] = halves(block, 1)
    weight = jnp.concatenate(
        [weights[at, rows, :] for at in range(2) for rows in (first, second)], axis=0
    )
    outs = []
    for step in range(steps):
        rows = pl.ds(step * chunk, chunk)
        left = jnp.concatenate(
            [orb[rows, :], orb_oth[rows, :], pair[rows, :], pair_oth[rows, :]], axis=1
        )
        high, low = split(left)
        wide = dot(high, weight)
        result[rows, :] += wide[:, :width] + wide[:, width:] + dot(low, weight[:, :width])
        copy = pltpu.make_async_copy(result.at[rows], out_hbm.at[rows], sems.at[step])
        copy.start()
        outs.append(copy)
    for copy in outs:
        copy.wait()


def limit(mib):
    return pltpu.CompilerParams(vmem_limit_bytes=mib * MIB)


def own_gram(orbitals, applied, cotangent):
    cells, width = orbitals.shape
    steps = cells // GRAM_CHUNK
    return pl.pallas_call(
        own_kernel,
        out_shape=(
            jax.ShapeDtypeStruct((width, width), F32),
            jax.ShapeDtypeStruct((steps, 2 * width, GRAM_CHUNK), BF16),
            jax.ShapeDtypeStruct((cells, width), F32),
            jax.ShapeDtypeStruct((2 * cells, width), F32),
        ),
        in_specs=[HBM] * 3,
        out_specs=(VMEM,) * 4,
        scratch_shapes=[pltpu.SemaphoreType.DMA((steps + 1, 2))],
        compiler_params=limit(12),
        cost_estimate=pl.CostEstimate(
            flops=8 * cells * width * width, bytes_accessed=3 * 4 * cells * width, transcendentals=0
        ),
        name="own_gram",
    )(orbitals, applied, cotangent)


def whole_gram(own, cot_t, orb_oth, near):
    cells, width = orb_oth.shape
    return pl.pallas_call(
        other_kernel,
        out_shape=jax.ShapeDtypeStruct((near, 2 * width // near, width), F32),
        in_specs=[VMEM, VMEM, VMEM],
        out_specs=VMEM,
        compiler_params=limit(10),
        name="whole_gram",
    )(own, cot_t, orb_oth)


def spread(parts, panel, receivers):
    near, tile, width = parts.shape
    return pl.pallas_call(
        spread_kernel,
        out_shape=jax.ShapeDtypeStruct((receivers, tile + OCTET, width), F32),
        in_specs=[VMEM, VMEM],
        out_specs=VMEM,
        compiler_params=limit(2),
        name="spread",
    )(parts, panel)


def gather(parts, receivers):
    far, rows, width = parts.shape
    return pl.pallas_call(
        gather_kernel,
        out_shape=jax.ShapeDtypeStruct((receivers, rows + OCTET, width), F32),
        in_specs=[VMEM],
        out_specs=VMEM,
        compiler_params=limit(2),
        name="gather",
    )(parts)


def tail(whole, levels, orb, pair, orb_oth, pair_oth):
    cells, width = orb.shape
    bands = 2 * width
    steps = cells // TAIL_CHUNK
    return pl.pallas_call(
        tail_kernel,
        out_shape=jax.ShapeDtypeStruct((cells, width), F32),
        in_specs=[VMEM] * 6,
        out_specs=HBM,
        scratch_shapes=[
            pltpu.VMEM((cells, width), F32),
            pltpu.VMEM((3, bands, bands), BF16),
            pltpu.SemaphoreType.DMA((steps,)),
        ],
        compiler_params=limit(20),
        name="tail",
    )(whole, levels.reshape(1, bands), orb, pair, orb_oth, pair_oth)


def body(orbitals, applied, cotangent, panel, levels):
    width = orbitals.shape[1]
    swap = [(0, 1), (1, 0)]
    near = lax.axis_size(NEAR)
    groups = far_groups()
    far = len(groups[0])

    blocks = [pltpu.with_memory_space_constraint(x, pltpu.HBM) for x in (orbitals, applied, cotangent)]
    orb_oth = lax.ppermute(orbitals, "bcol", swap)
    own, cot_t, orb, pair = own_gram(*blocks)
    pair, own, cot_t = lax.optimization_barrier((pair, own, cot_t))
    pair_oth = lax.ppermute(pair, "bcol", swap)
    partial = whole_gram(own, cot_t, orb_oth, near)
    parts = lax.all_to_all(partial, NEAR, 0, 0, tiled=True)
    parts = lax.all_to_all(
        spread(parts, panel, far), CELLS, 0, 0, tiled=True, axis_index_groups=groups
    )
    sums = lax.all_to_all(gather(parts, near), NEAR, 0, 0, tiled=True)
    whole = lax.all_gather(sums.reshape(-1, width), "bcol", axis=1, tiled=True)
    return tail(whole, levels, orb, pair, orb_oth, pair_oth)


def solution(mesh):
    fine = Mesh(mesh.devices.reshape(4, 2, 4, 4, 2, 2), ("zf", "zn", "x", "yf", "yn", "bcol"))
    cells = P(CELLS, "bcol")
    return jax.shard_map(
        body,
        mesh=fine,
        in_specs=(cells, cells, cells, P(("yf", "yn"), "bcol"), P()),
        out_specs=cells,
        check_vma=False,
    )
```

```python
import itertools

import jax
import jax.numpy as jnp
from jax import lax
from jax.experimental import pallas as pl
from jax.experimental.pallas import tpu as pltpu
from jax.sharding import Mesh
from jax.sharding import PartitionSpec as P

F32 = jnp.float32
BF16 = jnp.bfloat16
VMEM = pl.BlockSpec(memory_space=pltpu.VMEM)
HBM = pl.BlockSpec(memory_space=pltpu.HBM)
GRAM_CHUNK = 1152
TAIL_CHUNK = 576
INNER = ((1,), (0,))
NEAR = ("zn", "x", "yn")
CELLS = ("zf", "zn", "x", "yf", "yn")
QUARTET = 4
OCTET = 8
MIB = 2**20


def dot(left, right, dims=INNER, precision=None):
    return lax.dot_general(
        left, right, (dims, ((), ())), preferred_element_type=F32, precision=precision
    )


def far_groups():
    return [
        [
            (2 * zf + zn) * 32 + x * 8 + 2 * yf + (yn + yf // 2) % 2
            for zf, yf in itertools.product(range(4), range(4))
        ]
        for zn, x, yn in itertools.product(range(2), range(4), range(2))
    ]


def upper():
    return lax.axis_index("yf") // 2


def place(tile, mirror):
    return tile - mirror if tile % 2 else tile + mirror


def split(x):
    high = x.astype(BF16)
    return high, (x - high.astype(F32)).astype(BF16)


def product(left, right, dims=INNER):
    return dot(left[0], right[0], dims) + (dot(left[1], right[0], dims) + dot(left[0], right[1], dims))


def halves(x, axis):
    return jnp.concatenate(split(x), axis=axis)


def folded(total):
    rows, columns = total.shape[0] // 2, total.shape[1] // 2
    top, bottom = total[:rows], total[rows:]
    return (top[:, :columns] + top[:, columns:]) + (bottom[:, :columns] + bottom[:, columns:])


def own_kernel(
    orb_hbm, app_hbm, cot_hbm, out_ref, cot_t_ref, orb, pair, sems
):
    cells = orb.shape[0]
    steps = cot_t_ref.shape[0]
    chunk = cells // steps
    copies = []
    for step in range(steps):
        rows = pl.ds(step * chunk, chunk)
        below = pl.ds(cells + step * chunk, chunk)
        group = [
            pltpu.make_async_copy(orb_hbm.at[rows], orb.at[rows], sems.at[step, 0]),
            pltpu.make_async_copy(cot_hbm.at[rows], pair.at[below], sems.at[step, 1]),
        ]
        for copy in group:
            copy.start()
        copies.append(group)
    last = pltpu.make_async_copy(app_hbm, pair.at[pl.ds(0, cells)], sems.at[steps, 0])
    last.start()
    total = None
    for step in range(steps):
        for copy in copies[step]:
            copy.wait()
        cot_t = halves(pair[pl.ds(cells + step * chunk, chunk), :].T, 0)
        cot_t_ref[step] = cot_t
        part = dot(cot_t, halves(orb[pl.ds(step * chunk, chunk), :], 1))
        total = part if total is None else total + part
    out_ref[...] = folded(total)
    last.wait()


def other_kernel(own_ref, cot_t_ref, orb_ref, out_ref):
    steps = cot_t_ref.shape[0]
    chunk = orb_ref.shape[0] // steps
    width = own_ref.shape[0]
    total = None
    for step in range(steps):
        part = dot(cot_t_ref[step], halves(orb_ref[pl.ds(step * chunk, chunk), :], 1))
        total = part if total is None else total + part
    other = folded(total)
    first = lax.axis_index("bcol") == 0
    parts = (jnp.where(first, own_ref[...], other), jnp.where(first, other, own_ref[...]))
    rows = jnp.concatenate(parts, axis=0)
    mirror = upper()
    tile = out_ref.shape[1]
    for at in range(out_ref.shape[0]):
        out_ref[place(at, mirror)] = rows[at * tile : (at + 1) * tile, :]


def spread_kernel(parts_ref, panel_ref, out_ref):
    total = jnp.sum(parts_ref[...], axis=0)
    shape = (out_ref.shape[0],) + out_ref.shape[2:]
    last = out_ref.shape[1] - 1
    for at in range(last):
        out_ref[:, at] = jnp.broadcast_to(total[at * QUARTET : (at + 1) * QUARTET, :][None], shape)
    x = lax.axis_index("x")
    octet = panel_ref[pl.ds(pl.multiple_of((2 * lax.axis_index("zn") + x // 2) * OCTET, OCTET), OCTET), :]
    quartet = jnp.where(x % 2 == 0, octet[:QUARTET, :], octet[QUARTET:, :])
    out_ref[:, last] = jnp.broadcast_to(quartet[None], shape)


def gather_kernel(parts_ref, out_ref, block):
    last = parts_ref.shape[1] - 1
    for at in range(last):
        block[at * QUARTET : (at + 1) * QUARTET, :] = jnp.sum(parts_ref[:, at], axis=0)
    for yf in range(4):
        start = (last + yf) * QUARTET
        block[start : start + QUARTET, :] = parts_ref[yf, last]
    out_ref[...] = jnp.broadcast_to(block[...][None], out_ref.shape)


def tail_kernel(
    whole_ref, row_ref, orb, pair, orb_oth, pair_oth, out_hbm, result, weights, sems
):
    cells, width = result.shape
    steps = sems.shape[0]
    chunk = cells // steps
    mine = lax.axis_index("bcol")
    bands = 2 * width
    first = pl.ds(pl.multiple_of(mine * width, width), width)
    second = pl.ds(pl.multiple_of((1 - mine) * width, width), width)
    block = 4 * OCTET
    tile = 2 * OCTET
    mirror = upper()
    starts = [pl.multiple_of(place(at, mirror) * block, block) for at in range(bands // tile)]
    sums = jnp.concatenate([whole_ref[pl.ds(start, tile), :] for start in starts], axis=0)
    octets = []
    above = lax.broadcasted_iota(jnp.int32, (OCTET, bands), 0) < QUARTET
    for y in range(bands // block):
        yf = y // 2
        yn = (y + yf // 2) % 2
        for octet in range(block // OCTET):
            near = 8 * (octet // 2) + 4 * (octet % 2) + yn
            first_quartet, second_quartet = (
                whole_ref[pl.ds(pl.multiple_of(starts[at] + (tile + yf // 2 * OCTET), OCTET), OCTET), :]
                for at in (near, near + 2)
            )
            if yf % 2:
                first_quartet = pltpu.roll(first_quartet, QUARTET, 0)
            else:
                second_quartet = pltpu.roll(second_quartet, QUARTET, 0)
            octets.append(jnp.where(above, first_quartet, second_quartet))
    half = len(octets) // 2
    top, bottom = (jnp.concatenate(part, axis=0) for part in (octets[:half], octets[half:]))
    grad_t = jnp.concatenate(
        [
            jnp.concatenate(
                [sums[b * width : (b + 1) * width, c * width : (c + 1) * width] for b in range(2)],
                axis=1,
            )
            for c in range(2)
        ],
        axis=0,
    )
    rotation = split(jnp.concatenate([top, bottom], axis=0))
    rot_rows = jnp.where(mine == 0, top, bottom)
    weights[2] = halves(rot_rows.T, 1)
    weight = jnp.concatenate([weights[2, first, :], weights[2, second, :]], axis=0)

    def rotated(step):
        below = pl.ds(cells + step * chunk, chunk)
        high, low = split(jnp.concatenate([pair[below, :], pair_oth[below, :]], axis=1))
        wide = dot(high, weight)
        rows = pl.ds(step * chunk, chunk)
        result[rows, :] = wide[:, :width] + wide[:, width:] + dot(low, weight[:, :width])

    gram_t = product(split(grad_t), rotation)
    rotated(0)
    at_row = lax.broadcasted_iota(jnp.int32, (bands, bands), 0)
    at_col = lax.broadcasted_iota(jnp.int32, (bands, bands), 1)
    diagonal = at_row == at_col
    levels_row = jnp.broadcast_to(row_ref[...], (bands, bands))
    levels_col = levels_row.T
    gaps = jnp.where(diagonal, 1.0, levels_col - levels_row)
    mixing_t = jnp.where(diagonal, 0.0, (1.0 / gaps) * gram_t)
    sym_ham = mixing_t + mixing_t.T
    scaled = levels_col * mixing_t
    sym_ovl = scaled + scaled.T + jnp.where(diagonal, gram_t, 0.0)
    right = product(
        split(jnp.concatenate([sym_ovl, sym_ham], axis=0)), split(rot_rows), ((1,), (1,))
    )
    rotated(1)
    coefs = product(rotation, split(jnp.concatenate([-right[:bands], right[bands:]], axis=1)))
    for step in range(2, steps):
        rotated(step)
    for at, block in enumerate((coefs[:, :width], coefs[:, width:])):
        weights[at] = halves(block, 1)
    weight = jnp.concatenate(
        [weights[at, rows, :] for at in range(2) for rows in (first, second)], axis=0
    )
    outs = []
    for step in range(steps):
        rows = pl.ds(step * chunk, chunk)
        left = jnp.concatenate(
            [orb[rows, :], orb_oth[rows, :], pair[rows, :], pair_oth[rows, :]], axis=1
        )
        high, low = split(left)
        wide = dot(high, weight)
        result[rows, :] += wide[:, :width] + wide[:, width:] + dot(low, weight[:, :width])
        copy = pltpu.make_async_copy(result.at[rows], out_hbm.at[rows], sems.at[step])
        copy.start()
        outs.append(copy)
    for copy in outs:
        copy.wait()


def limit(mib):
    return pltpu.CompilerParams(vmem_limit_bytes=mib * MIB)


def own_gram(orbitals, applied, cotangent):
    cells, width = orbitals.shape
    steps = cells // GRAM_CHUNK
    return pl.pallas_call(
        own_kernel,
        out_shape=(
            jax.ShapeDtypeStruct((width, width), F32),
            jax.ShapeDtypeStruct((steps, 2 * width, GRAM_CHUNK), BF16),
            jax.ShapeDtypeStruct((cells, width), F32),
            jax.ShapeDtypeStruct((2 * cells, width), F32),
        ),
        in_specs=[HBM] * 3,
        out_specs=(VMEM,) * 4,
        scratch_shapes=[pltpu.SemaphoreType.DMA((steps + 1, 2))],
        compiler_params=limit(12),
        cost_estimate=pl.CostEstimate(
            flops=8 * cells * width * width, bytes_accessed=3 * 4 * cells * width, transcendentals=0
        ),
        name="own_gram",
    )(orbitals, applied, cotangent)


def whole_gram(own, cot_t, orb_oth, near):
    cells, width = orb_oth.shape
    return pl.pallas_call(
        other_kernel,
        out_shape=jax.ShapeDtypeStruct((near, 2 * width // near, width), F32),
        in_specs=[VMEM, VMEM, VMEM],
        out_specs=VMEM,
        compiler_params=limit(10),
        cost_estimate=pl.CostEstimate(flops=8 * cells * width * width, bytes_accessed=8 * cells * width, transcendentals=0),
        name="whole_gram",
    )(own, cot_t, orb_oth)


def spread(parts, panel, receivers):
    near, tile, width = parts.shape
    return pl.pallas_call(
        spread_kernel,
        out_shape=jax.ShapeDtypeStruct((receivers, tile // QUARTET + 1, QUARTET, width), F32),
        in_specs=[VMEM, VMEM],
        out_specs=VMEM,
        compiler_params=limit(2),
        name="spread",
    )(parts, panel)


def gather(parts, receivers):
    far, quartets, rows, width = parts.shape
    height = (quartets - 1 + 4) * rows
    return pl.pallas_call(
        gather_kernel,
        out_shape=jax.ShapeDtypeStruct((receivers, height, width), F32),
        in_specs=[VMEM],
        out_specs=VMEM,
        scratch_shapes=[pltpu.VMEM((height, width), F32)],
        compiler_params=limit(2),
        name="gather",
    )(parts)


def tail(whole, levels, orb, pair, orb_oth, pair_oth):
    cells, width = orb.shape
    bands = 2 * width
    steps = cells // TAIL_CHUNK
    return pl.pallas_call(
        tail_kernel,
        out_shape=jax.ShapeDtypeStruct((cells, width), F32),
        in_specs=[VMEM] * 6,
        out_specs=HBM,
        scratch_shapes=[
            pltpu.VMEM((cells, width), F32),
            pltpu.VMEM((3, bands, bands), BF16),
            pltpu.SemaphoreType.DMA((steps,)),
        ],
        compiler_params=limit(20),
        name="tail",
    )(whole, levels.reshape(1, bands), orb, pair, orb_oth, pair_oth)


def body(orbitals, applied, cotangent, panel, levels):
    width = orbitals.shape[1]
    swap = [(0, 1), (1, 0)]
    near = lax.axis_size(NEAR)
    groups = far_groups()
    far = len(groups[0])

    blocks = [pltpu.with_memory_space_constraint(x, pltpu.HBM) for x in (orbitals, applied, cotangent)]
    orb_oth = lax.ppermute(orbitals, "bcol", swap)
    own, cot_t, orb, pair = own_gram(*blocks)
    pair, own, cot_t = lax.optimization_barrier((pair, own, cot_t))
    pair_oth = lax.ppermute(pair, "bcol", swap)
    partial = whole_gram(own, cot_t, orb_oth, near)
    parts = lax.all_to_all(partial, NEAR, 0, 0, tiled=True)
    parts = lax.all_to_all(
        spread(parts, panel, far), CELLS, 0, 0, tiled=True, axis_index_groups=groups
    )
    sums = lax.all_to_all(gather(parts, near), NEAR, 0, 0, tiled=True)
    whole = lax.all_gather(sums.reshape(-1, width), "bcol", axis=1, tiled=True)
    return tail(whole, levels, orb, pair, orb_oth, pair_oth)


def solution(mesh):
    fine = Mesh(mesh.devices.reshape(4, 2, 4, 4, 2, 2), ("zf", "zn", "x", "yf", "yn", "bcol"))
    cells = P(CELLS, "bcol")
    return jax.shard_map(
        body,
        mesh=fine,
        in_specs=(cells, cells, cells, P(("yf", "yn"), "bcol"), P()),
        out_specs=cells,
        check_vma=False,
    )
```

```python
import itertools

import jax
import jax.numpy as jnp
from jax import lax
from jax.experimental import pallas as pl
from jax.experimental.pallas import tpu as pltpu
from jax.sharding import Mesh
from jax.sharding import PartitionSpec as P

F32 = jnp.float32
BF16 = jnp.bfloat16
VMEM = pl.BlockSpec(memory_space=pltpu.VMEM)
HBM = pl.BlockSpec(memory_space=pltpu.HBM)
GRAM_CHUNK = 1152
TAIL_CHUNK = 576
INNER = ((1,), (0,))
NEAR = ("zn", "x", "yn")
CELLS = ("zf", "zn", "x", "yf", "yn")
OCTET = 8
MIB = 2**20


def dot(left, right, dims=INNER, precision=None):
    return lax.dot_general(
        left, right, (dims, ((), ())), preferred_element_type=F32, precision=precision
    )


def far_groups():
    return [
        [
            (2 * zf + zn) * 32 + x * 8 + 2 * yf + (yn + yf // 2) % 2
            for zf, yf in itertools.product((2, 1, 3, 0), range(4))
        ]
        for zn, x, yn in itertools.product(range(2), range(4), range(2))
    ]


def upper():
    return lax.axis_index("yf") // 2


def place(tile, mirror):
    return tile - mirror if tile % 2 else tile + mirror


def split(x):
    high = x.astype(BF16)
    return high, (x - high.astype(F32)).astype(BF16)


def product(left, right, dims=INNER):
    return dot(left[0], right[0], dims) + (dot(left[1], right[0], dims) + dot(left[0], right[1], dims))


def halves(x, axis):
    return jnp.concatenate(split(x), axis=axis)


def folded(total):
    rows, columns = total.shape[0] // 2, total.shape[1] // 2
    top, bottom = total[:rows], total[rows:]
    return (top[:, :columns] + top[:, columns:]) + (bottom[:, :columns] + bottom[:, columns:])


def own_kernel(
    orb_hbm, app_hbm, cot_hbm, out_ref, cot_t_ref, orb, pair, sems
):
    cells = orb.shape[0]
    steps = cot_t_ref.shape[0]
    chunk = cells // steps
    copies = []
    for step in range(steps):
        rows = pl.ds(step * chunk, chunk)
        below = pl.ds(cells + step * chunk, chunk)
        group = [
            pltpu.make_async_copy(orb_hbm.at[rows], orb.at[rows], sems.at[step, 0]),
            pltpu.make_async_copy(cot_hbm.at[rows], pair.at[below], sems.at[step, 1]),
        ]
        for copy in group:
            copy.start()
        copies.append(group)
    last = pltpu.make_async_copy(app_hbm, pair.at[pl.ds(0, cells)], sems.at[steps, 0])
    last.start()
    total = None
    for step in range(steps):
        for copy in copies[step]:
            copy.wait()
        cot_t = halves(pair[pl.ds(cells + step * chunk, chunk), :].T, 0)
        cot_t_ref[step] = cot_t
        part = dot(cot_t, halves(orb[pl.ds(step * chunk, chunk), :], 1))
        total = part if total is None else total + part
    out_ref[...] = folded(total)
    last.wait()


def other_kernel(own_ref, cot_t_ref, orb_ref, out_ref):
    steps = cot_t_ref.shape[0]
    chunk = orb_ref.shape[0] // steps
    width = own_ref.shape[0]
    total = None
    for step in range(steps):
        part = dot(cot_t_ref[step], halves(orb_ref[pl.ds(step * chunk, chunk), :], 1))
        total = part if total is None else total + part
    other = folded(total)
    first = lax.axis_index("bcol") == 0
    parts = (jnp.where(first, own_ref[...], other), jnp.where(first, other, own_ref[...]))
    rows = jnp.concatenate(parts, axis=0)
    mirror = upper()
    tile = out_ref.shape[1]
    for at in range(out_ref.shape[0]):
        out_ref[place(at, mirror)] = rows[at * tile : (at + 1) * tile, :]


def spread_kernel(parts_ref, panel_ref, out_ref):
    octet = pl.ds(pl.multiple_of(lax.axis_index("x") * OCTET, OCTET), OCTET)
    both = jnp.concatenate([jnp.sum(parts_ref[...], axis=0), panel_ref[octet, :]], axis=0)
    out_ref[...] = jnp.broadcast_to(both[None], out_ref.shape)


def gather_kernel(parts_ref, out_ref):
    tile = parts_ref.shape[1] - OCTET
    octets = parts_ref[pl.ds(2 * lax.axis_index("zn"), 2), tile:, :]
    total = jnp.sum(parts_ref[:, :tile, :], axis=0)
    both = jnp.concatenate([total, octets.reshape(2 * OCTET, total.shape[1])], axis=0)
    out_ref[...] = jnp.broadcast_to(both[None], out_ref.shape)


def tail_kernel(
    whole_ref, row_ref, orb, pair, orb_oth, pair_oth, out_hbm, result, weights, sems
):
    cells, width = result.shape
    steps = sems.shape[0]
    chunk = cells // steps
    mine = lax.axis_index("bcol")
    bands = 2 * width
    first = pl.ds(pl.multiple_of(mine * width, width), width)
    second = pl.ds(pl.multiple_of((1 - mine) * width, width), width)
    block = 4 * OCTET
    tile = 2 * OCTET
    mirror = upper()
    starts = [pl.multiple_of(place(at, mirror) * block, block) for at in range(bands // tile)]
    sums = jnp.concatenate([whole_ref[pl.ds(start, tile), :] for start in starts], axis=0)
    octets = []
    for y in range(bands // block):
        zn, slot = y // 4, y // 2 % 2
        yn = (y + zn) % 2
        for x in range(block // OCTET):
            start = starts[8 * zn + 2 * x + yn] + (tile + slot * OCTET)
            octets.append(whole_ref[pl.ds(pl.multiple_of(start, OCTET), OCTET), :])
    half = len(octets) // 2
    top, bottom = (jnp.concatenate(part, axis=0) for part in (octets[:half], octets[half:]))
    grad_t = jnp.concatenate(
        [
            jnp.concatenate(
                [sums[b * width : (b + 1) * width, c * width : (c + 1) * width] for b in range(2)],
                axis=1,
            )
            for c in range(2)
        ],
        axis=0,
    )
    rotation = split(jnp.concatenate([top, bottom], axis=0))
    rot_rows = jnp.where(mine == 0, top, bottom)
    weights[2] = halves(rot_rows.T, 1)
    weight = jnp.concatenate([weights[2, first, :], weights[2, second, :]], axis=0)

    def rotated(step):
        below = pl.ds(cells + step * chunk, chunk)
        high, low = split(jnp.concatenate([pair[below, :], pair_oth[below, :]], axis=1))
        wide = dot(high, weight)
        rows = pl.ds(step * chunk, chunk)
        result[rows, :] = wide[:, :width] + wide[:, width:] + dot(low, weight[:, :width])

    gram_t = product(split(grad_t), rotation)
    rotated(0)
    at_row = lax.broadcasted_iota(jnp.int32, (bands, bands), 0)
    at_col = lax.broadcasted_iota(jnp.int32, (bands, bands), 1)
    diagonal = at_row == at_col
    levels_row = jnp.broadcast_to(row_ref[...], (bands, bands))
    levels_col = levels_row.T
    gaps = jnp.where(diagonal, 1.0, levels_col - levels_row)
    mixing_t = jnp.where(diagonal, 0.0, (1.0 / gaps) * gram_t)
    sym_ham = mixing_t + mixing_t.T
    scaled = levels_col * mixing_t
    sym_ovl = scaled + scaled.T + jnp.where(diagonal, gram_t, 0.0)
    right = product(
        split(jnp.concatenate([sym_ovl, sym_ham], axis=0)), split(rot_rows), ((1,), (1,))
    )
    rotated(1)
    coefs = product(rotation, split(jnp.concatenate([-right[:bands], right[bands:]], axis=1)))
    for step in range(2, steps):
        rotated(step)
    for at, block in enumerate((coefs[:, :width], coefs[:, width:])):
        weights[at] = halves(block, 1)
    weight = jnp.concatenate(
        [weights[at, rows, :] for at in range(2) for rows in (first, second)], axis=0
    )
    outs = []
    for step in range(steps):
        rows = pl.ds(step * chunk, chunk)
        left = jnp.concatenate(
            [orb[rows, :], orb_oth[rows, :], pair[rows, :], pair_oth[rows, :]], axis=1
        )
        high, low = split(left)
        wide = dot(high, weight)
        result[rows, :] += wide[:, :width] + wide[:, width:] + dot(low, weight[:, :width])
        copy = pltpu.make_async_copy(result.at[rows], out_hbm.at[rows], sems.at[step])
        copy.start()
        outs.append(copy)
    for copy in outs:
        copy.wait()


def limit(mib):
    return pltpu.CompilerParams(vmem_limit_bytes=mib * MIB)


def own_gram(orbitals, applied, cotangent):
    cells, width = orbitals.shape
    steps = cells // GRAM_CHUNK
    return pl.pallas_call(
        own_kernel,
        out_shape=(
            jax.ShapeDtypeStruct((width, width), F32),
            jax.ShapeDtypeStruct((steps, 2 * width, GRAM_CHUNK), BF16),
            jax.ShapeDtypeStruct((cells, width), F32),
            jax.ShapeDtypeStruct((2 * cells, width), F32),
        ),
        in_specs=[HBM] * 3,
        out_specs=(VMEM,) * 4,
        scratch_shapes=[pltpu.SemaphoreType.DMA((steps + 1, 2))],
        compiler_params=limit(12),
        cost_estimate=pl.CostEstimate(
            flops=8 * cells * width * width, bytes_accessed=3 * 4 * cells * width, transcendentals=0
        ),
        name="own_gram",
    )(orbitals, applied, cotangent)


def whole_gram(own, cot_t, orb_oth, near):
    cells, width = orb_oth.shape
    return pl.pallas_call(
        other_kernel,
        out_shape=jax.ShapeDtypeStruct((near, 2 * width // near, width), F32),
        in_specs=[VMEM, VMEM, VMEM],
        out_specs=VMEM,
        compiler_params=limit(10),
        name="whole_gram",
    )(own, cot_t, orb_oth)


def spread(parts, panel, receivers):
    near, tile, width = parts.shape
    return pl.pallas_call(
        spread_kernel,
        out_shape=jax.ShapeDtypeStruct((receivers, tile + OCTET, width), F32),
        in_specs=[VMEM, VMEM],
        out_specs=VMEM,
        compiler_params=limit(2),
        name="spread",
    )(parts, panel)


def gather(parts, receivers):
    far, rows, width = parts.shape
    return pl.pallas_call(
        gather_kernel,
        out_shape=jax.ShapeDtypeStruct((receivers, rows + OCTET, width), F32),
        in_specs=[VMEM],
        out_specs=VMEM,
        compiler_params=limit(2),
        name="gather",
    )(parts)


def tail(whole, levels, orb, pair, orb_oth, pair_oth):
    cells, width = orb.shape
    bands = 2 * width
    steps = cells // TAIL_CHUNK
    return pl.pallas_call(
        tail_kernel,
        out_shape=jax.ShapeDtypeStruct((cells, width), F32),
        in_specs=[VMEM] * 6,
        out_specs=HBM,
        scratch_shapes=[
            pltpu.VMEM((cells, width), F32),
            pltpu.VMEM((3, bands, bands), BF16),
            pltpu.SemaphoreType.DMA((steps,)),
        ],
        compiler_params=limit(20),
        name="tail",
    )(whole, levels.reshape(1, bands), orb, pair, orb_oth, pair_oth)


def body(orbitals, applied, cotangent, panel, levels):
    width = orbitals.shape[1]
    swap = [(0, 1), (1, 0)]
    near = lax.axis_size(NEAR)
    groups = far_groups()
    far = len(groups[0])

    blocks = [pltpu.with_memory_space_constraint(x, pltpu.HBM) for x in (orbitals, applied, cotangent)]
    orb_oth = lax.ppermute(orbitals, "bcol", swap)
    own, cot_t, orb, pair = own_gram(*blocks)
    pair, own, cot_t = lax.optimization_barrier((pair, own, cot_t))
    pair_oth = lax.ppermute(pair, "bcol", swap)
    partial = whole_gram(own, cot_t, orb_oth, near)
    parts = lax.all_to_all(partial, NEAR, 0, 0, tiled=True)
    parts = lax.all_to_all(
        spread(parts, panel, far), CELLS, 0, 0, tiled=True, axis_index_groups=groups
    )
    sums = lax.all_to_all(gather(parts, near), NEAR, 0, 0, tiled=True)
    whole = lax.all_gather(sums.reshape(-1, width), "bcol", axis=1, tiled=True)
    return tail(whole, levels, orb, pair, orb_oth, pair_oth)


def solution(mesh):
    fine = Mesh(mesh.devices.reshape(4, 2, 4, 4, 2, 2), ("zf", "zn", "x", "yf", "yn", "bcol"))
    cells = P(CELLS, "bcol")
    return jax.shard_map(
        body,
        mesh=fine,
        in_specs=(cells, cells, cells, P(("yf", "yn"), "bcol"), P()),
        out_specs=cells,
        check_vma=False,
    )
```

```python
import itertools

import jax
import jax.numpy as jnp
from jax import lax
from jax.experimental import pallas as pl
from jax.experimental.pallas import tpu as pltpu
from jax.sharding import Mesh
from jax.sharding import PartitionSpec as P

F32 = jnp.float32
BF16 = jnp.bfloat16
VMEM = pl.BlockSpec(memory_space=pltpu.VMEM)
HBM = pl.BlockSpec(memory_space=pltpu.HBM)
GRAM_CHUNK = 1152
TAIL_CHUNK = 576
INNER = ((1,), (0,))
NEAR = ("zn", "x", "yn")
CELLS = ("zf", "zn", "x", "yf", "yn")
OCTET = 8
MIB = 2**20


def dot(left, right, dims=INNER, precision=None):
    return lax.dot_general(
        left, right, (dims, ((), ())), preferred_element_type=F32, precision=precision
    )


def far_groups():
    return [
        [
            (2 * zf + zn) * 32 + x * 8 + 2 * yf + (yn + yf // 2) % 2
            for zf, yf in itertools.product((2, 1, 3, 0), (2, 1, 3, 0))
        ]
        for zn, x, yn in itertools.product(range(2), range(4), range(2))
    ]


def upper():
    return lax.axis_index("yf") // 2


def place(tile, mirror):
    return tile - mirror if tile % 2 else tile + mirror


def split(x):
    high = x.astype(BF16)
    return high, (x - high.astype(F32)).astype(BF16)


def product(left, right, dims=INNER):
    return dot(left[0], right[0], dims) + (dot(left[1], right[0], dims) + dot(left[0], right[1], dims))


def halves(x, axis):
    return jnp.concatenate(split(x), axis=axis)


def folded(total):
    rows, columns = total.shape[0] // 2, total.shape[1] // 2
    top, bottom = total[:rows], total[rows:]
    return (top[:, :columns] + top[:, columns:]) + (bottom[:, :columns] + bottom[:, columns:])


def own_kernel(
    orb_hbm, app_hbm, cot_hbm, out_ref, cot_t_ref, orb, pair, sems
):
    cells = orb.shape[0]
    steps = cot_t_ref.shape[0]
    chunk = cells // steps
    copies = []
    for step in range(steps):
        rows = pl.ds(step * chunk, chunk)
        below = pl.ds(cells + step * chunk, chunk)
        group = [
            pltpu.make_async_copy(orb_hbm.at[rows], orb.at[rows], sems.at[step, 0]),
            pltpu.make_async_copy(cot_hbm.at[rows], pair.at[below], sems.at[step, 1]),
        ]
        for copy in group:
            copy.start()
        copies.append(group)
    last = pltpu.make_async_copy(app_hbm, pair.at[pl.ds(0, cells)], sems.at[steps, 0])
    last.start()
    total = None
    for step in range(steps):
        for copy in copies[step]:
            copy.wait()
        cot_t = halves(pair[pl.ds(cells + step * chunk, chunk), :].T, 0)
        cot_t_ref[step] = cot_t
        part = dot(cot_t, halves(orb[pl.ds(step * chunk, chunk), :], 1))
        total = part if total is None else total + part
    out_ref[...] = folded(total)
    last.wait()


def other_kernel(own_ref, cot_t_ref, orb_ref, out_ref):
    steps = cot_t_ref.shape[0]
    chunk = orb_ref.shape[0] // steps
    width = own_ref.shape[0]
    total = None
    for step in range(steps):
        part = dot(cot_t_ref[step], halves(orb_ref[pl.ds(step * chunk, chunk), :], 1))
        total = part if total is None else total + part
    other = folded(total)
    first = lax.axis_index("bcol") == 0
    parts = (jnp.where(first, own_ref[...], other), jnp.where(first, other, own_ref[...]))
    rows = jnp.concatenate(parts, axis=0)
    mirror = upper()
    tile = out_ref.shape[1]
    for at in range(out_ref.shape[0]):
        out_ref[place(at, mirror)] = rows[at * tile : (at + 1) * tile, :]


def spread_kernel(parts_ref, panel_ref, out_ref):
    octet = pl.ds(pl.multiple_of(lax.axis_index("x") * OCTET, OCTET), OCTET)
    both = jnp.concatenate([jnp.sum(parts_ref[...], axis=0), panel_ref[octet, :]], axis=0)
    out_ref[...] = jnp.broadcast_to(both[None], out_ref.shape)


def gather_kernel(parts_ref, out_ref):
    tile = parts_ref.shape[1] - OCTET
    zn = lax.axis_index("zn")
    octets = jnp.stack([parts_ref[3 - 3 * zn, tile:, :], parts_ref[1 + zn, tile:, :]])
    total = jnp.sum(parts_ref[:, :tile, :], axis=0)
    both = jnp.concatenate([total, octets.reshape(2 * OCTET, total.shape[1])], axis=0)
    out_ref[...] = jnp.broadcast_to(both[None], out_ref.shape)


def tail_kernel(
    whole_ref, row_ref, orb, pair, orb_oth, pair_oth, out_hbm, result, weights, sems
):
    cells, width = result.shape
    steps = sems.shape[0]
    chunk = cells // steps
    mine = lax.axis_index("bcol")
    bands = 2 * width
    first = pl.ds(pl.multiple_of(mine * width, width), width)
    second = pl.ds(pl.multiple_of((1 - mine) * width, width), width)
    block = 4 * OCTET
    tile = 2 * OCTET
    mirror = upper()
    starts = [pl.multiple_of(place(at, mirror) * block, block) for at in range(bands // tile)]
    sums = jnp.concatenate([whole_ref[pl.ds(start, tile), :] for start in starts], axis=0)
    octets = []
    for y in range(bands // block):
        zn, slot = y // 4, y // 2 % 2
        yn = (y + zn) % 2
        for x in range(block // OCTET):
            start = starts[8 * zn + 2 * x + yn] + (tile + slot * OCTET)
            octets.append(whole_ref[pl.ds(pl.multiple_of(start, OCTET), OCTET), :])
    half = len(octets) // 2
    top, bottom = (jnp.concatenate(part, axis=0) for part in (octets[:half], octets[half:]))
    grad_t = jnp.concatenate(
        [
            jnp.concatenate(
                [sums[b * width : (b + 1) * width, c * width : (c + 1) * width] for b in range(2)],
                axis=1,
            )
            for c in range(2)
        ],
        axis=0,
    )
    rotation = split(jnp.concatenate([top, bottom], axis=0))
    rot_rows = jnp.where(mine == 0, top, bottom)
    weights[2] = halves(rot_rows.T, 1)
    weight = jnp.concatenate([weights[2, first, :], weights[2, second, :]], axis=0)

    def rotated(step):
        below = pl.ds(cells + step * chunk, chunk)
        high, low = split(jnp.concatenate([pair[below, :], pair_oth[below, :]], axis=1))
        wide = dot(high, weight)
        rows = pl.ds(step * chunk, chunk)
        result[rows, :] = wide[:, :width] + wide[:, width:] + dot(low, weight[:, :width])

    gram_t = product(split(grad_t), rotation)
    rotated(0)
    at_row = lax.broadcasted_iota(jnp.int32, (bands, bands), 0)
    at_col = lax.broadcasted_iota(jnp.int32, (bands, bands), 1)
    diagonal = at_row == at_col
    levels_row = jnp.broadcast_to(row_ref[...], (bands, bands))
    levels_col = levels_row.T
    gaps = jnp.where(diagonal, 1.0, levels_col - levels_row)
    mixing_t = jnp.where(diagonal, 0.0, (1.0 / gaps) * gram_t)
    sym_ham = mixing_t + mixing_t.T
    scaled = levels_col * mixing_t
    sym_ovl = scaled + scaled.T + jnp.where(diagonal, gram_t, 0.0)
    right = product(
        split(jnp.concatenate([sym_ovl, sym_ham], axis=0)), split(rot_rows), ((1,), (1,))
    )
    rotated(1)
    coefs = product(rotation, split(jnp.concatenate([-right[:bands], right[bands:]], axis=1)))
    for step in range(2, steps):
        rotated(step)
    for at, block in enumerate((coefs[:, :width], coefs[:, width:])):
        weights[at] = halves(block, 1)
    weight = jnp.concatenate(
        [weights[at, rows, :] for at in range(2) for rows in (first, second)], axis=0
    )
    outs = []
    for step in range(steps):
        rows = pl.ds(step * chunk, chunk)
        left = jnp.concatenate(
            [orb[rows, :], orb_oth[rows, :], pair[rows, :], pair_oth[rows, :]], axis=1
        )
        high, low = split(left)
        wide = dot(high, weight)
        result[rows, :] += wide[:, :width] + wide[:, width:] + dot(low, weight[:, :width])
        copy = pltpu.make_async_copy(result.at[rows], out_hbm.at[rows], sems.at[step])
        copy.start()
        outs.append(copy)
    for copy in outs:
        copy.wait()


def limit(mib):
    return pltpu.CompilerParams(vmem_limit_bytes=mib * MIB)


def own_gram(orbitals, applied, cotangent):
    cells, width = orbitals.shape
    steps = cells // GRAM_CHUNK
    return pl.pallas_call(
        own_kernel,
        out_shape=(
            jax.ShapeDtypeStruct((width, width), F32),
            jax.ShapeDtypeStruct((steps, 2 * width, GRAM_CHUNK), BF16),
            jax.ShapeDtypeStruct((cells, width), F32),
            jax.ShapeDtypeStruct((2 * cells, width), F32),
        ),
        in_specs=[HBM] * 3,
        out_specs=(VMEM,) * 4,
        scratch_shapes=[pltpu.SemaphoreType.DMA((steps + 1, 2))],
        compiler_params=limit(12),
        cost_estimate=pl.CostEstimate(
            flops=8 * cells * width * width, bytes_accessed=3 * 4 * cells * width, transcendentals=0
        ),
        name="own_gram",
    )(orbitals, applied, cotangent)


def whole_gram(own, cot_t, orb_oth, near):
    cells, width = orb_oth.shape
    return pl.pallas_call(
        other_kernel,
        out_shape=jax.ShapeDtypeStruct((near, 2 * width // near, width), F32),
        in_specs=[VMEM, VMEM, VMEM],
        out_specs=VMEM,
        compiler_params=limit(10),
        name="whole_gram",
    )(own, cot_t, orb_oth)


def spread(parts, panel, receivers):
    near, tile, width = parts.shape
    return pl.pallas_call(
        spread_kernel,
        out_shape=jax.ShapeDtypeStruct((receivers, tile + OCTET, width), F32),
        in_specs=[VMEM, VMEM],
        out_specs=VMEM,
        compiler_params=limit(2),
        name="spread",
    )(parts, panel)


def gather(parts, receivers):
    far, rows, width = parts.shape
    return pl.pallas_call(
        gather_kernel,
        out_shape=jax.ShapeDtypeStruct((receivers, rows + OCTET, width), F32),
        in_specs=[VMEM],
        out_specs=VMEM,
        compiler_params=limit(2),
        name="gather",
    )(parts)


def tail(whole, levels, orb, pair, orb_oth, pair_oth):
    cells, width = orb.shape
    bands = 2 * width
    steps = cells // TAIL_CHUNK
    return pl.pallas_call(
        tail_kernel,
        out_shape=jax.ShapeDtypeStruct((cells, width), F32),
        in_specs=[VMEM] * 6,
        out_specs=HBM,
        scratch_shapes=[
            pltpu.VMEM((cells, width), F32),
            pltpu.VMEM((3, bands, bands), BF16),
            pltpu.SemaphoreType.DMA((steps,)),
        ],
        compiler_params=limit(20),
        name="tail",
    )(whole, levels.reshape(1, bands), orb, pair, orb_oth, pair_oth)


def body(orbitals, applied, cotangent, panel, levels):
    width = orbitals.shape[1]
    swap = [(0, 1), (1, 0)]
    near = lax.axis_size(NEAR)
    groups = far_groups()
    far = len(groups[0])

    blocks = [pltpu.with_memory_space_constraint(x, pltpu.HBM) for x in (orbitals, applied, cotangent)]
    orb_oth = lax.ppermute(orbitals, "bcol", swap)
    own, cot_t, orb, pair = own_gram(*blocks)
    pair, own, cot_t = lax.optimization_barrier((pair, own, cot_t))
    pair_oth = lax.ppermute(pair, "bcol", swap)
    partial = whole_gram(own, cot_t, orb_oth, near)
    parts = lax.all_to_all(partial, NEAR, 0, 0, tiled=True)
    parts = lax.all_to_all(
        spread(parts, panel, far), CELLS, 0, 0, tiled=True, axis_index_groups=groups
    )
    sums = lax.all_to_all(gather(parts, near), NEAR, 0, 0, tiled=True)
    whole = lax.all_gather(sums.reshape(-1, width), "bcol", axis=1, tiled=True)
    return tail(whole, levels, orb, pair, orb_oth, pair_oth)


def solution(mesh):
    fine = Mesh(mesh.devices.reshape(4, 2, 4, 4, 2, 2), ("zf", "zn", "x", "yf", "yn", "bcol"))
    cells = P(CELLS, "bcol")
    return jax.shard_map(
        body,
        mesh=fine,
        in_specs=(cells, cells, cells, P(("yf", "yn"), "bcol"), P()),
        out_specs=cells,
        check_vma=False,
    )
```
